128 devices in a mesh: pipe: 4 (over y), expert: 32 (over z, x, core).
Axes of the slice: x: 4, y: 4, z: 4, core: 2. Of those that a mesh axis runs over, the one named last changes fastest.
Arguments:
- acts: bfloat16 [4, 4096, 3072], P('pipe', 'expert'), may hold values from -6 to 6
- hid_grad: bfloat16 [4, 4096, 2, 8192], P('pipe', 'expert'), may hold values from -6 to 6
- routes: int32 [4, 4096, 2], P('pipe', 'expert'), may hold values from 0 to 7, all different within a row; in each aligned block of 128 rows (0 to 127, 128 to 255, ..., all dimensions but the last counted through in order) at most 64 rows name the same one
- probs: float32 [4, 4096, 2], P('pipe', 'expert'), may hold values from 0.1 to 0.9
- w_gate: bfloat16 [4, 32, 3072, 2048], P('pipe', 'expert'), may hold values from -0.109375 to 0.109375
Outputs:
- in_grad: bfloat16 [4, 4096, 3072], P('pipe', 'expert')
The draws below stay inside these ranges and needn't reach their ends.
Inputs may be any that keep to these rules, and one draw needn't show every extreme that they name: `routes`: each token names 2 different experts. Among the 128 tokens of one device in one section, no expert is named more than 64 times, and in every draw some device names some expert exactly 64 times.
All inputs are finite; a program needn't handle non-finite values.
Results may differ from the reference program's by a relative error of at most 0.013.
Values may be sent and summed in bfloat16 or wider, within the bound.
No kernel may reach another device: no remote copies, remote signals or barrier semaphores. Data moves between devices by JAX's collectives and lax.ppermute only.
A program may use at most 192 MiB of HBM per device.

```python
import math
import jax
import jax.numpy as jnp
import numpy as np
from jax import lax

D = 3072
HID_DEV = 2048
EXPERTS = 8
TOP = 2
TOK_DEV = 128
SLOTS = 64
SHARDS = 4
FF = 8192
TOKENS = 4096
SEGMENTS = 4
N_EXPERT = 32


def levels(rng, shape, split, least, top_value):
    loudness = 1.0
    for dim, blocks in split:
        steps = jax.random.uniform(jax.random.fold_in(jax.random.fold_in(rng, 6), dim), (blocks,), jnp.float32, least / len(split), top_value / len(split))
        loudness = loudness * jnp.repeat(jnp.exp(steps), shape[dim] // blocks).reshape((-1,) + (1,) * (len(shape) - 1 - dim))
    return loudness


def routed_block(rng, own, number, rows, amount, top, reach, lean):
    ranking = jax.random.permutation(rng, amount)
    heavy_load, ordinary = load_shares(amount, rows * top, reach, lean, True), load_shares(amount, rows * top, reach, lean, False)
    places = jnp.arange(amount)

    def named(tallies, rotation):
        used = int((tallies > 0).sum())
        fixed = max(1, used // 4)
        shifted = fixed + (places - fixed + rotation * (used - fixed)) % max(1, amount - fixed)
        return jnp.zeros((amount,), jnp.int32).at[ranking[jnp.where(places < fixed, places, shifted)]].set(jnp.asarray(tallies, jnp.int32))

    tallies = jnp.where(number % 4 == 0, named(heavy_load, number // 4), named(ordinary, number - number // 4 - 1))
    mixed = jax.random.permutation(jax.random.fold_in(own, 3), amount)
    giver, taker = mixed[0:amount // 2 * 2:2], mixed[1:amount // 2 * 2:2]
    slack = jnp.minimum(tallies[giver] - 1, reach - tallies[taker]) // 2
    slack = jnp.where((giver == ranking[0]) | (taker == ranking[0]) | (tallies[taker] == 0), 0, jnp.maximum(slack, 0))
    shifted = jax.random.randint(jax.random.fold_in(own, 4), (amount // 2,), 0, 1 << 20) % (slack + 1)
    tallies = tallies.at[giver].add(-shifted).at[taker].add(shifted)
    items = jnp.searchsorted(jnp.cumsum(tallies), jnp.arange(rows * top), side="right").astype(jnp.int32)
    table = items.reshape(top, rows).T
    table = table[jax.random.permutation(jax.random.fold_in(own, 1), rows)]
    rotation = jax.random.randint(jax.random.fold_in(own, 2), (rows, 1), 0, top)
    return jnp.take_along_axis(table, (jnp.arange(top)[None, :] + rotation) % top, axis=1)


def load_shares(number_of, total, limit, skew, full):
    loads = [(1 << 20) // math.isqrt(standing ** skew) + 1 for standing in range(1, number_of + 1)]
    largest = limit if full else min(limit, max(-(-total // number_of), total * loads[0] // sum(loads)))
    least = 1 if total - largest >= number_of - 1 else 0
    holding, surplus = [largest] + [least] * (number_of - 1), total - largest - least * (number_of - 1)
    while surplus > 0:
        candidates = [i for i in range(1, number_of) if holding[i] < largest] or [i for i in range(1, number_of) if holding[i] < limit]
        whole, left = sum([loads[i] for i in candidates]), surplus
        for i in candidates:
            extra = min(limit - holding[i], max(1, left * loads[i] // whole), surplus)
            holding[i] = holding[i] + extra
            surplus = surplus - extra
    return np.array(holding)


def normal_values(key, dims, scale, most, cuts=(), kind=jnp.bfloat16):
    result = jax.random.normal(key, dims, jnp.float32) * scale
    if len(cuts) > 0:
        result = levels(key, dims, cuts, -0.22, 0.18) * result
    return jnp.clip(result, min=-most, max=most).astype(kind)


def setup_inputs(seed: int = 0) -> dict:
    arg_keys = jax.random.split(jax.random.key(seed), 6)
    acts = normal_values(arg_keys[0], (SEGMENTS, TOKENS, D), 1.0, 6.0, ((0, 4), (1, 32)))
    hid_grad = normal_values(arg_keys[1], (SEGMENTS, TOKENS, TOP, FF), 1.0, 6.0, ((0, 4), (1, 32)))
    routes_keys = jax.random.split(jax.random.fold_in(arg_keys[2], 1), SEGMENTS * TOKENS // TOK_DEV)
    routes_turns = jax.random.permutation(jax.random.fold_in(arg_keys[2], 3), SEGMENTS * TOKENS // TOK_DEV)
    routes = jax.vmap(lambda own, number: routed_block(jax.random.fold_in(arg_keys[2], 2), own, number, TOK_DEV, EXPERTS, TOP, SLOTS, 2))(routes_keys, routes_turns).reshape((SEGMENTS, TOKENS, TOP))
    probs = jnp.clip(0.1 + 0.79999997 * jax.random.uniform(arg_keys[3], (SEGMENTS, TOKENS, TOP), jnp.float32) ** levels(arg_keys[3], (SEGMENTS, TOKENS, TOP), ((0, 4), (1, 32)), -0.2, 0.2), 0.1, 0.9)
    w_gate = normal_values(arg_keys[4], (SEGMENTS, N_EXPERT, D, HID_DEV), D ** -0.5, 0.109375, ((0, 4), (1, 32)))
    return dict(acts=acts, hid_grad=hid_grad, routes=routes, probs=probs, w_gate=w_gate)


def expert_rows(rows_in, grads_in, gate_part):
    rows_wide = rows_in.astype(jnp.float32)
    gate_wide = gate_part.astype(jnp.float32)
    gate_pre = jnp.einsum('rd,fdh->rfh', rows_wide, gate_wide)
    grad_hidden = grads_in.astype(jnp.float32).reshape(rows_in.shape[0], SHARDS, HID_DEV)
    squash = jax.nn.sigmoid(gate_pre)
    derivative = squash * (1.0 + gate_pre * (1.0 - squash))
    grad_gate = (grad_hidden * derivative).astype(jnp.bfloat16)
    shard_term = jnp.einsum('rfh,fdh->rfd', grad_gate.astype(jnp.float32), gate_wide).astype(jnp.bfloat16)
    return lax.optimization_barrier(jnp.sum(shard_term.astype(jnp.float32), axis=1))

def section_grad(tokens_in, arrived, route_table, weight_table, gate_all):
    pairs = TOKENS * TOP
    route_grads = arrived.reshape(pairs, FF)
    flat_expert = route_table.reshape(-1).astype(jnp.int32)
    order = jnp.argsort(flat_expert, stable=True).astype(jnp.int32)
    onehot_table = (flat_expert[:, None] == jnp.arange(EXPERTS, dtype=jnp.int32)[None, :]).astype(jnp.int32)
    counts = lax.optimization_barrier(jnp.sum(onehot_table, axis=0)).astype(jnp.int32)
    padded = (counts + 127) // 128 * 128
    padded_start = jnp.cumsum(padded) - padded
    plain_start = jnp.cumsum(counts) - counts
    sorted_expert = flat_expert[order]
    place = padded_start[sorted_expert] + jnp.arange(pairs, dtype=jnp.int32) - plain_start[sorted_expert]
    tile_count = (pairs + 127) // 128 + EXPERTS
    table = jnp.full((tile_count * 128,), pairs, jnp.int32).at[place.astype(jnp.int32)].set(order)
    tile_start = jnp.arange(tile_count, dtype=jnp.int32) * 128
    tile_expert = lax.optimization_barrier(jnp.sum(((padded_start + padded)[None, :] <= tile_start[:, None]).astype(jnp.int32), axis=1))
    tile_expert = jnp.minimum(tile_expert, EXPERTS - 1).astype(jnp.int32)
    gate_split = gate_all.reshape(EXPERTS, SHARDS, D, HID_DEV)

    def one_tile(operands):
        pair_index, expert_id = operands
        safe_pair = jnp.minimum(pair_index, pairs - 1)
        token_id = safe_pair // TOP
        return expert_rows(tokens_in[token_id], route_grads[safe_pair], gate_split[expert_id])
    results = lax.map(one_tile, (table.reshape(tile_count, 128), tile_expert))
    returned = jnp.zeros((pairs, D), jnp.float32).at[table].set(results.reshape(-1, D), mode='drop')
    return lax.optimization_barrier(jnp.sum(returned.reshape(TOKENS, TOP, D) * weight_table[:, :, None], axis=1)).astype(jnp.bfloat16)

def reference(acts, hid_grad, routes, probs, w_gate):
    computed = []
    for section in range(SEGMENTS):
        computed.append(section_grad(acts[section], hid_grad[(section + 1) % SEGMENTS], routes[section], probs[section], w_gate[section]))
    return jnp.stack([computed[(section + 1) % SEGMENTS] for section in range(SEGMENTS)])
```

```python
import jax
import jax.numpy as jnp
from jax import lax
from jax.sharding import Mesh, PartitionSpec as P

EXPERTS = 8
TOP = 2
SLOTS = 64
PLANE = ("p", "z", "xp")
BACK = [((i + 1) % 4, i) for i in range(4)]
COLUMN_PARTS = 2


def exchange(block):
    return lax.all_to_all(block, PLANE, split_axis=0, concat_axis=0, tiled=True)


def derivative(gate_pre):
    squash = jax.nn.sigmoid(gate_pre)
    return (squash * (1.0 + gate_pre * (1.0 - squash))).astype(jnp.bfloat16)


def bf16_dot(a, b, dims):
    return lax.dot_general(a, b, (dims, ((), ())), preferred_element_type=jnp.float32)


def local(acts, hid_grad, routes, probs, w_gate):
    tokens = acts[0]
    n_tokens, width = tokens.shape
    mine = w_gate[0, 0]
    hidden = mine.shape[1]
    core = lax.axis_index("core")
    arrived = lax.ppermute(hid_grad[0], "pipe", BACK)
    other = lax.ppermute(mine, "core", [(0, 1), (1, 0)])

    flat_expert = routes[0].reshape(-1)
    pairs = flat_expert.shape[0]
    number = jnp.arange(pairs, dtype=jnp.int32)
    earlier = (flat_expert[:, None] == flat_expert[None, :]) & (number[None, :] < number[:, None])
    slot = jnp.sum(earlier.astype(jnp.int32), axis=1)
    target = flat_expert * SLOTS + slot
    places = jnp.arange(EXPERTS * SLOTS, dtype=jnp.int32)
    place_pair = (places[:, None] == target[None, :]).astype(jnp.bfloat16)
    by_token = target.reshape(n_tokens, TOP)
    token_hit = [places[:, None] == by_token[None, :, k] for k in range(TOP)]
    place_token = (token_hit[0] | token_hit[1]).astype(jnp.bfloat16)

    sent_rows = bf16_dot(place_token, tokens, ((1,), (0,))).astype(jnp.bfloat16)
    sent_rows = jnp.broadcast_to(
        sent_rows.reshape(1, EXPERTS, SLOTS, width), (2, EXPERTS, SLOTS, width)
    ).reshape(2 * EXPERTS, SLOTS, width)
    rows = exchange(sent_rows).reshape(-1, width)

    grads = arrived.reshape(pairs, 2, 2, hidden)
    received = []
    for half in range(2):
        shard = lax.rem(core + half, 2)
        piece = lax.dynamic_index_in_dim(grads, shard, 2, keepdims=False)
        placed = [
            bf16_dot(place_pair, piece[:, p], ((1,), (0,))).astype(jnp.bfloat16) for p in range(2)
        ]
        sent = jnp.stack(placed).reshape(2 * EXPERTS, SLOTS, hidden)
        received.append(exchange(sent).reshape(-1, hidden))

    weights = (mine, other)
    gate = [
        received[half].astype(jnp.float32)
        * derivative(bf16_dot(rows, weights[half], ((1,), (0,)))).astype(jnp.float32)
        for half in range(2)
    ]
    gate = [g.astype(jnp.bfloat16) for g in gate]

    hit = [by_token[:, k, None] == places[None, :] for k in range(TOP)]
    mix = sum(jnp.where(hit[k], probs[0][:, k, None], 0.0) for k in range(TOP))
    high = lax.reduce_precision(mix, 8, 7)
    low = mix - high
    mix = jnp.concatenate([high, low]).astype(jnp.bfloat16)
    mix = jnp.concatenate([mix, mix], axis=1)

    cut = width // COLUMN_PARTS
    parts = []
    for j in range(COLUMN_PARTS):
        term = sum(
            bf16_dot(gate[half], weights[half][j * cut : (j + 1) * cut], ((1,), (1,)))
            for half in range(2)
        )
        sent = term.astype(jnp.bfloat16).reshape(2 * EXPERTS, SLOTS, cut)
        returned = exchange(sent).reshape(-1, cut)
        both = bf16_dot(mix, returned, ((1,), (0,)))
        summed = (both[:n_tokens] + both[n_tokens:]).astype(jnp.bfloat16)
        parts.append(lax.ppermute(summed, "pipe", BACK))
    return jnp.concatenate(parts, axis=1)[None]


def solution(mesh):
    fine = Mesh(mesh.devices.reshape(4, 4, 2, 2, 2), ("pipe", "z", "xp", "p", "core"))
    expert = ("z", "xp", "p", "core")
    placed = (
        P("pipe", expert, None),
        P("pipe", expert, None, None),
        P("pipe", expert, None),
        P("pipe", expert, None),
        P("pipe", expert, None, None),
    )
    return jax.shard_map(
        local, mesh=fine, in_specs=placed, out_specs=P("pipe", expert, None), check_vma=False
    )
```

```python
import jax
import jax.numpy as jnp
from jax import lax
from jax.experimental import pallas as pl
from jax.experimental.pallas import tpu as pltpu
from jax.sharding import Mesh, PartitionSpec as P

EXPERTS = 8
TOP = 2
SLOTS = 64
HALF = SLOTS // 2
SHARDS = 4
PLANE = ("p", "z", "xp")
BACK = [((i + 1) % 4, i) for i in range(4)]
AHEAD = [(i, (i + 1) % 4) for i in range(4)]
PLACE_COLUMNS = 512


def exchange(block):
    return lax.all_to_all(block, PLANE, split_axis=0, concat_axis=0, tiled=True)


def derivative(gate_pre):
    squash = jax.nn.sigmoid(gate_pre)
    return (squash * (1.0 + gate_pre * (1.0 - squash))).astype(jnp.bfloat16)


def bf16_dot(a, b, dims):
    return lax.dot_general(a, b, (dims, ((), ())), preferred_element_type=jnp.float32)


def place_kernel(target_ref, grads_ref, *refs):
    outs = refs[-2:]
    pairs = grads_ref.shape[0]
    places = lax.broadcasted_iota(jnp.int32, (EXPERTS * SLOTS, pairs), 0)
    hit = jnp.where(places == target_ref[...], 1.0, 0.0).astype(jnp.bfloat16)
    placed = jnp.dot(hit, grads_ref[...], preferred_element_type=jnp.float32)
    placed = placed.astype(jnp.bfloat16)
    for e in range(EXPERTS):
        for half in range(2):
            start = e * SLOTS + half * HALF
            outs[half][e] = placed[start : start + HALF]


def place(target, quarter, f, buffers):
    pairs, hidden = quarter.shape
    steps = hidden // PLACE_COLUMNS
    shape = jax.ShapeDtypeStruct((2 * EXPERTS, HALF, 2 * hidden), jnp.bfloat16)
    spot = pl.BlockSpec(
        (EXPERTS, HALF, PLACE_COLUMNS), lambda j: (f // 2, 0, (f % 2) * steps + j)
    )
    return pl.pallas_call(
        place_kernel,
        grid=(steps,),
        in_specs=[
            pl.BlockSpec((1, pairs), lambda j: (0, 0)),
            pl.BlockSpec((pairs, PLACE_COLUMNS), lambda j: (0, j)),
        ]
        + [pl.BlockSpec(memory_space=pl.ANY)] * len(buffers),
        out_specs=[spot, spot],
        out_shape=[shape, shape],
        input_output_aliases={2 + i: i for i in range(len(buffers))},
        compiler_params=pltpu.CompilerParams(vmem_limit_bytes=32 * 1024 * 1024),
        cost_estimate=pl.CostEstimate(
            flops=2 * EXPERTS * SLOTS * pairs * hidden,
            bytes_accessed=2 * (EXPERTS * SLOTS + pairs) * hidden,
            transcendentals=0,
        ),
        name=f"place_quarter_{f}",
    )(target.reshape(1, pairs), quarter, *buffers)


def local(acts, hid_grad, routes, probs, w_gate):
    tokens = acts[0]
    n_tokens, width = tokens.shape
    mine = w_gate[0, 0]
    hidden = mine.shape[1]
    core = lax.axis_index("core")

    flat_expert = routes[0].reshape(-1)
    pairs = flat_expert.shape[0]
    quarters = [
        hid_grad[0][:, :, f * hidden : (f + 1) * hidden].reshape(pairs, hidden)
        for f in range(SHARDS)
    ]
    for _ in range(3):
        quarters[3] = lax.ppermute(quarters[3], "pipe", AHEAD)
    for f in range(3):
        quarters[f] = lax.ppermute(quarters[f], "pipe", BACK)
    other = lax.ppermute(mine, "core", [(0, 1), (1, 0)])

    number = jnp.arange(pairs, dtype=jnp.int32)
    earlier = (flat_expert[:, None] == flat_expert[None, :]) & (number[None, :] < number[:, None])
    slot = jnp.sum(earlier.astype(jnp.int32), axis=1)
    target = flat_expert * SLOTS + slot
    by_token = target.reshape(n_tokens, TOP)

    places = jnp.arange(EXPERTS * SLOTS, dtype=jnp.int32)
    token_hit = [places[:, None] == by_token[None, :, k] for k in range(TOP)]
    place_token = (token_hit[0] | token_hit[1]).astype(jnp.bfloat16)
    sent_rows = bf16_dot(place_token, tokens, ((1,), (0,))).astype(jnp.bfloat16)
    sent_rows = jnp.broadcast_to(
        sent_rows.reshape(1, EXPERTS, SLOTS, width), (2, EXPERTS, SLOTS, width)
    ).reshape(2 * EXPERTS, SLOTS, width)
    rows = exchange(sent_rows).reshape(-1, width)

    buffers = []
    for f in range(SHARDS):
        buffers = place(target, quarters[f], f, buffers)
    received = [exchange(buffer) for buffer in buffers]

    weights = (mine, other)
    slopes = [
        lax.optimization_barrier(derivative(bf16_dot(rows, w, ((1,), (0,))))) for w in weights
    ]
    slopes = [slope.reshape(2 * EXPERTS, 2, HALF, hidden) for slope in slopes]

    total = 0.0
    for half in range(2):
        term = 0.0
        for part in range(2):
            shard = lax.rem(core + part, 2)
            grads = lax.dynamic_slice_in_dim(received[half], shard * hidden, hidden, 2)
            gate = grads.astype(jnp.float32) * slopes[part][:, half].astype(jnp.float32)
            gate = gate.astype(jnp.bfloat16).reshape(2 * EXPERTS * HALF, hidden)
            term = term + bf16_dot(gate, weights[part], ((1,), (1,)))
        sent = term.astype(jnp.bfloat16).reshape(2 * EXPERTS, HALF, width)
        returned = exchange(sent).reshape(2 * EXPERTS * HALF, width)

        here = places.reshape(EXPERTS, 2, HALF)[:, half].reshape(-1)
        hit = [by_token[:, k, None] == here[None, :] for k in range(TOP)]
        mix = sum(jnp.where(hit[k], probs[0][:, k, None], 0.0) for k in range(TOP))
        high = lax.reduce_precision(mix, 8, 7)
        mix = jnp.concatenate([high, mix - high]).astype(jnp.bfloat16)
        mix = jnp.concatenate([mix, mix], axis=1)
        both = bf16_dot(mix, returned, ((1,), (0,)))
        total = total + both[:n_tokens] + both[n_tokens:]
    return lax.ppermute(total.astype(jnp.bfloat16), "pipe", BACK)[None]


def solution(mesh):
    fine = Mesh(mesh.devices.reshape(4, 4, 2, 2, 2), ("pipe", "z", "xp", "p", "core"))
    expert = ("z", "xp", "p", "core")
    placed = (
        P("pipe", expert, None),
        P("pipe", expert, None, None),
        P("pipe", expert, None),
        P("pipe", expert, None),
        P("pipe", expert, None, None),
    )
    return jax.shard_map(
        local, mesh=fine, in_specs=placed, out_specs=P("pipe", expert, None), check_vma=False
    )
```

```python
import jax
import jax.numpy as jnp
from jax import lax
from jax.experimental import pallas as pl
from jax.experimental.pallas import tpu as pltpu
from jax.sharding import Mesh, PartitionSpec as P

EXPERTS = 8
TOP = 2
SLOTS = 64
PLANE = ("z", "xp", "p", "core")
DEVICES = 32
SHARE = SLOTS // 2
BACK = [((i + 1) % 4, i) for i in range(4)]
COLUMN_PARTS = 2
VMEM = 56 * 1024 * 1024


def exchange(block):
    return lax.all_to_all(block, PLANE, split_axis=0, concat_axis=0, tiled=True)


def derivative(gate_pre):
    squash = jax.nn.sigmoid(gate_pre)
    return (squash * (1.0 + gate_pre * (1.0 - squash))).astype(jnp.bfloat16)


def bf16_dot(a, b, dims):
    return lax.dot_general(a, b, (dims, ((), ())), preferred_element_type=jnp.float32)


def place_kernel(target_ref, grads_ref, out_ref):
    tokens, top, columns = grads_ref.shape
    places = lax.broadcasted_iota(jnp.int32, (EXPERTS * SLOTS, tokens * top), 0)
    hit = jnp.where(places == target_ref[...], 1.0, 0.0).astype(jnp.bfloat16)
    grads = grads_ref[...].reshape(tokens * top, columns)
    placed = jnp.dot(hit, grads, preferred_element_type=jnp.float32).astype(jnp.bfloat16)
    out_ref[:, 0] = placed.reshape(EXPERTS, 2, SHARE, columns)


def place(target, grads):
    tokens, top, width = grads.shape
    pairs, hidden = tokens * top, width // 2
    columns = 1024
    steps = hidden // columns
    out = pl.pallas_call(
        place_kernel,
        grid=(2, steps),
        in_specs=[
            pl.BlockSpec((1, pairs), lambda p, j: (0, 0)),
            pl.BlockSpec((tokens, top, columns), lambda p, j: (0, 0, p * steps + j)),
        ],
        out_specs=pl.BlockSpec((EXPERTS, 1, 2, SHARE, columns), lambda p, j: (0, p, 0, 0, j)),
        out_shape=jax.ShapeDtypeStruct((EXPERTS, 2, 2, SHARE, hidden), jnp.bfloat16),
        compiler_params=pltpu.CompilerParams(vmem_limit_bytes=VMEM),
        cost_estimate=pl.CostEstimate(
            flops=4 * EXPERTS * SLOTS * pairs * hidden,
            bytes_accessed=4 * (EXPERTS * SLOTS + pairs) * hidden,
            transcendentals=0,
        ),
        name="place_grads",
    )(target.reshape(1, pairs), grads)
    return out.reshape(DEVICES, SHARE, hidden)


SOURCES = 4


def pick_kernel(base_ref, target_ref, tokens_ref, out_ref):
    n_tokens = tokens_ref.shape[1]
    wanted = base_ref[0] + lax.broadcasted_iota(jnp.int32, (SHARE, n_tokens), 0)
    for i in range(SOURCES):
        hit = (wanted == target_ref[i, 0:1]) | (wanted == target_ref[i, 1:2])
        hit = jnp.where(hit, 1.0, 0.0).astype(jnp.bfloat16)
        rows = jnp.dot(hit, tokens_ref[i], preferred_element_type=jnp.float32)
        out_ref[i] = rows.astype(jnp.bfloat16)


def pick(base, targets, tokens):
    sources, n_tokens, width = tokens.shape
    return pl.pallas_call(
        pick_kernel,
        grid=(sources // SOURCES,),
        in_specs=[
            pl.BlockSpec(memory_space=pltpu.SMEM),
            pl.BlockSpec((SOURCES, TOP, n_tokens), lambda i: (i, 0, 0)),
            pl.BlockSpec((SOURCES, n_tokens, width), lambda i: (i, 0, 0)),
        ],
        out_specs=pl.BlockSpec((SOURCES, SHARE, width), lambda i: (i, 0, 0)),
        out_shape=jax.ShapeDtypeStruct((sources, SHARE, width), jnp.bfloat16),
        compiler_params=pltpu.CompilerParams(vmem_limit_bytes=VMEM),
        cost_estimate=pl.CostEstimate(
            flops=2 * sources * SHARE * n_tokens * width,
            bytes_accessed=2 * sources * (SHARE + n_tokens) * width,
            transcendentals=0,
        ),
        name="pick_rows",
    )(base.reshape(1), targets, tokens)


DEEP = 1024


def term_kernel(g0, g1, s0, s1, w0, w1, out_ref, gate, total):
    j, k = pl.program_id(0), pl.program_id(1)

    @pl.when(j == 0)
    def _():
        for half, (g, s) in enumerate(((g0, s0), (g1, s1))):
            product = g[...].astype(jnp.float32) * s[...].astype(jnp.float32)
            gate[2 * k + half] = product.astype(jnp.bfloat16)

    def part(half, w):
        return bf16_dot(gate[2 * k + half], w[...], ((1,), (1,)))

    @pl.when(k == 0)
    def _():
        total[...] = part(0, w0) + part(1, w1)

    @pl.when(k == 1)
    def _():
        out_ref[...] = (total[...] + part(0, w0) + part(1, w1)).astype(jnp.bfloat16)


def terms(grads, slopes, weights, first, columns):
    rows, hidden = grads[0].shape
    wide = 768
    steps, offset = columns // wide, first // wide
    side = pl.BlockSpec((rows, DEEP), lambda j, k: (0, jnp.where(j == 0, k, 1)))
    weight = pl.BlockSpec((wide, DEEP), lambda j, k: (offset + j, k))
    return pl.pallas_call(
        term_kernel,
        grid=(steps, hidden // DEEP),
        in_specs=[side] * 4 + [weight] * 2,
        out_specs=pl.BlockSpec((rows, wide), lambda j, k: (0, j)),
        out_shape=jax.ShapeDtypeStruct((rows, columns), jnp.bfloat16),
        scratch_shapes=[
            pltpu.VMEM((4, rows, DEEP), jnp.bfloat16),
            pltpu.VMEM((rows, wide), jnp.float32),
        ],
        compiler_params=pltpu.CompilerParams(vmem_limit_bytes=VMEM),
        cost_estimate=pl.CostEstimate(
            flops=4 * rows * hidden * columns,
            bytes_accessed=8 * rows * hidden + 4 * hidden * columns + 2 * rows * columns,
            transcendentals=0,
        ),
        name="terms",
    )(*grads, *slopes, *weights)


def local(acts, hid_grad, routes, probs, w_gate):
    tokens = acts[0]
    n_tokens, width = tokens.shape
    mine = w_gate[0, 0]
    hidden = mine.shape[1]
    core = lax.axis_index("core")
    expert = lax.axis_index("z") * 2 + lax.axis_index("xp")

    halves = []
    for h in range(2):
        pieces = [hid_grad[0][:, :, f * hidden : (f + 1) * hidden] for f in (h, 2 + h)]
        halves.append(lax.ppermute(jnp.concatenate(pieces, axis=2), "pipe", BACK))
    gathered = lax.all_gather(tokens, PLANE, axis=0)
    other = lax.ppermute(mine, "core", [(0, 1), (1, 0)])

    flat_expert = routes[0].reshape(-1)
    pairs = flat_expert.shape[0]
    number = jnp.arange(pairs, dtype=jnp.int32)
    earlier = (flat_expert[:, None] == flat_expert[None, :]) & (number[None, :] < number[:, None])
    slot = jnp.sum(earlier.astype(jnp.int32), axis=1)
    target = flat_expert * SLOTS + slot
    by_token = target.reshape(n_tokens, TOP)
    targets = lax.all_gather(by_token.T, PLANE, axis=0)

    received = []
    for h in range(2):
        received.append(exchange(place(target, halves[h])).reshape(DEVICES * SHARE, hidden))

    gathered, received[0] = lax.optimization_barrier((gathered, received[0]))
    weights = (jnp.where(core == 0, mine, other), jnp.where(core == 0, other, mine))
    rows = pick(expert * SLOTS + core * SHARE, targets, gathered).reshape(DEVICES * SHARE, width)
    slopes = [
        lax.optimization_barrier(derivative(bf16_dot(rows, w, ((1,), (0,))))) for w in weights
    ]

    places = jnp.arange(EXPERTS * SLOTS, dtype=jnp.int32).reshape(EXPERTS, 1, SLOTS)
    places = jnp.broadcast_to(places, (EXPERTS, 2, SLOTS)).reshape(-1)
    hit = [by_token[:, k, None] == places[None, :] for k in range(TOP)]
    mix = sum(jnp.where(hit[k], probs[0][:, k, None], 0.0) for k in range(TOP))
    high = lax.reduce_precision(mix, 8, 7)
    mix = jnp.concatenate([high, mix - high]).astype(jnp.bfloat16)

    columns = width // COLUMN_PARTS
    parts = []
    for j in range(COLUMN_PARTS):
        term = terms(received, slopes, weights, j * columns, columns)
        returned = exchange(term.reshape(DEVICES, SHARE, columns)).reshape(-1, columns)
        both = bf16_dot(mix, returned, ((1,), (0,)))
        summed = (both[:n_tokens] + both[n_tokens:]).astype(jnp.bfloat16)
        parts.append(lax.ppermute(summed, "pipe", BACK))
    return jnp.concatenate(parts, axis=1)[None]


def solution(mesh):
    fine = Mesh(mesh.devices.reshape(4, 4, 2, 2, 2), ("pipe",) + PLANE)
    placed = (
        P("pipe", PLANE, None),
        P("pipe", PLANE, None, None),
        P("pipe", PLANE, None),
        P("pipe", PLANE, None),
        P("pipe", PLANE, None, None),
    )
    return jax.shard_map(
        local, mesh=fine, in_specs=placed, out_specs=P("pipe", PLANE, None), check_vma=False
    )
```

```python
import functools

import jax
import jax.numpy as jnp
from jax import lax
from jax.experimental import pallas as pl
from jax.experimental.pallas import tpu as pltpu
from jax.sharding import Mesh, PartitionSpec as P

EXPERTS = 8
TOP = 2
SLOTS = 64
PLANE = ("z", "xp", "p", "core")
DEVICES = 32
SHARE = SLOTS // 2
BACK = [((i + 1) % 4, i) for i in range(4)]
COLUMN_PARTS = 2
VMEM = 56 * 1024 * 1024


def exchange(block):
    return lax.all_to_all(block, PLANE, split_axis=0, concat_axis=0, tiled=True)


def after(*values):
    return lax.optimization_barrier(values if len(values) > 1 else values[0])


def derivative(gate_pre):
    squash = jax.nn.sigmoid(gate_pre)
    return (squash * (1.0 + gate_pre * (1.0 - squash))).astype(jnp.bfloat16)


def bf16_dot(a, b, dims):
    return lax.dot_general(a, b, (dims, ((), ())), preferred_element_type=jnp.float32)


def place_kernel(target_ref, grads_ref, out_ref):
    tokens, top, columns = grads_ref.shape
    places = lax.broadcasted_iota(jnp.int32, (EXPERTS * SLOTS, tokens * top), 0)
    hit = jnp.where(places == target_ref[...], 1.0, 0.0).astype(jnp.bfloat16)
    grads = grads_ref[...].reshape(tokens * top, columns)
    placed = jnp.dot(hit, grads, preferred_element_type=jnp.float32).astype(jnp.bfloat16)
    out_ref[:, 0] = placed.reshape(EXPERTS, 2, SHARE, columns)


def place(target, grads):
    tokens, top, width = grads.shape
    pairs, hidden = tokens * top, width // 2
    columns = 1024
    steps = hidden // columns
    out = pl.pallas_call(
        place_kernel,
        grid=(2, steps),
        in_specs=[
            pl.BlockSpec((1, pairs), lambda p, j: (0, 0)),
            pl.BlockSpec((tokens, top, columns), lambda p, j: (0, 0, p * steps + j)),
        ],
        out_specs=pl.BlockSpec((EXPERTS, 1, 2, SHARE, columns), lambda p, j: (0, p, 0, 0, j)),
        out_shape=jax.ShapeDtypeStruct((EXPERTS, 2, 2, SHARE, hidden), jnp.bfloat16),
        compiler_params=pltpu.CompilerParams(vmem_limit_bytes=VMEM),
        cost_estimate=pl.CostEstimate(
            flops=4 * EXPERTS * SLOTS * pairs * hidden,
            bytes_accessed=4 * (EXPERTS * SLOTS + pairs) * hidden,
            transcendentals=0,
        ),
        name="place_grads",
    )(target.reshape(1, pairs), grads)
    return out.reshape(DEVICES, SHARE, hidden)


SOURCES = 4


def pick_kernel(base_ref, target_ref, tokens_ref, out_ref):
    n_tokens, width = tokens_ref.shape[1:]
    shape = (2 * SHARE, n_tokens)
    row = lax.broadcasted_iota(jnp.int32, shape, 0)
    wanted = base_ref[0] + lax.rem(row, SHARE)
    for i in range(0, SOURCES, 2):
        hits = []
        for n in range(2):
            hit = (wanted == target_ref[i + n, 0:1]) | (wanted == target_ref[i + n, 1:2])
            hit = hit & (row // SHARE == n)
            hits.append(jnp.where(hit, 1.0, 0.0).astype(jnp.bfloat16))
        both = tokens_ref[i : i + 2].reshape(2 * n_tokens, width)
        rows = jnp.dot(jnp.concatenate(hits, axis=1), both, preferred_element_type=jnp.float32)
        out_ref[i : i + 2] = rows.astype(jnp.bfloat16).reshape(2, SHARE, width)


def pick(base, targets, tokens):
    sources, n_tokens, width = tokens.shape
    return pl.pallas_call(
        pick_kernel,
        grid=(sources // SOURCES,),
        in_specs=[
            pl.BlockSpec(memory_space=pltpu.SMEM),
            pl.BlockSpec((SOURCES, TOP, n_tokens), lambda i: (i, 0, 0)),
            pl.BlockSpec((SOURCES, n_tokens, width), lambda i: (i, 0, 0)),
        ],
        out_specs=pl.BlockSpec((SOURCES, SHARE, width), lambda i: (i, 0, 0)),
        out_shape=jax.ShapeDtypeStruct((sources, SHARE, width), jnp.bfloat16),
        compiler_params=pltpu.CompilerParams(vmem_limit_bytes=VMEM),
        cost_estimate=pl.CostEstimate(
            flops=2 * sources * SHARE * n_tokens * width,
            bytes_accessed=2 * sources * (SHARE + n_tokens) * width,
            transcendentals=0,
        ),
        name="pick_rows",
    )(base.reshape(1), targets, tokens)


def copy_kernel(in_ref, out_ref):
    out_ref[...] = in_ref[...]


def cut(grads, h):
    tokens, top, width = grads.shape
    columns = width // 8
    return pl.pallas_call(
        copy_kernel,
        grid=(2, 2),
        in_specs=[
            pl.BlockSpec((tokens, top, columns), lambda p, j: (0, 0, (2 * p + h) * 2 + j)),
        ],
        out_specs=pl.BlockSpec((tokens, top, columns), lambda p, j: (0, 0, 2 * p + j)),
        out_shape=jax.ShapeDtypeStruct((tokens, top, width // 2), grads.dtype),
        compiler_params=pltpu.CompilerParams(vmem_limit_bytes=VMEM),
        cost_estimate=pl.CostEstimate(
            flops=0, bytes_accessed=2 * tokens * top * width, transcendentals=0
        ),
        name="cut_grads",
    )(grads)


DEEP = 512
WIDE = 768


def term_kernel(n, based, *refs):
    grads, slopes, weights = refs[:n], refs[n : 2 * n], refs[2 * n : 3 * n]
    out_ref, gate, total = refs[-3:]
    j, k = pl.program_id(0), pl.program_id(1)

    @pl.when(j == 0)
    def _():
        for i in range(n):
            product = grads[i][...].astype(jnp.float32) * slopes[i][...].astype(jnp.float32)
            gate[n * k + i] = product.astype(jnp.bfloat16)

    def step():
        return sum(bf16_dot(gate[n * k + i], weights[i][...], ((1,), (1,))) for i in range(n))

    last = pl.num_programs(1) - 1

    @pl.when(k == 0)
    def _():
        total[...] = step() + refs[3 * n][...] if based else step()

    @pl.when((k > 0) & (k < last))
    def _():
        total[...] += step()

    @pl.when(k == last)
    def _():
        out_ref[...] = (total[...] + step()).astype(out_ref.dtype)


def terms(grads, slopes, weights, first, columns, base=None, dtype=jnp.bfloat16):
    n = len(grads)
    rows, hidden = grads[0].shape
    steps, offset, depth = columns // WIDE, first // WIDE, hidden // DEEP
    side = pl.BlockSpec((rows, DEEP), lambda j, k: (0, jnp.where(j == 0, k, depth - 1)))
    weight = pl.BlockSpec((WIDE, DEEP), lambda j, k: (offset + j, k))
    column = pl.BlockSpec((rows, WIDE), lambda j, k: (0, j))
    behind = pl.BlockSpec((rows, WIDE), lambda j, k: (0, offset + j))
    based = base is not None
    return pl.pallas_call(
        functools.partial(term_kernel, n, based),
        grid=(steps, depth),
        in_specs=[side] * (2 * n) + [weight] * n + [behind] * based,
        out_specs=column,
        out_shape=jax.ShapeDtypeStruct((rows, columns), dtype),
        scratch_shapes=[
            pltpu.VMEM((n * depth, rows, DEEP), jnp.bfloat16),
            pltpu.VMEM((rows, WIDE), jnp.float32),
        ],
        compiler_params=pltpu.CompilerParams(vmem_limit_bytes=VMEM),
        cost_estimate=pl.CostEstimate(
            flops=2 * n * rows * hidden * columns,
            bytes_accessed=2 * n * hidden * (2 * rows + columns) + 4 * rows * columns,
            transcendentals=0,
        ),
        name="terms",
    )(*grads, *slopes, *weights, *([base] if based else []))


def local(acts, hid_grad, routes, probs, w_gate):
    tokens = acts[0]
    n_tokens, width = tokens.shape
    mine = w_gate[0, 0]
    hidden = mine.shape[1]
    core = lax.axis_index("core")
    expert = lax.axis_index("z") * 2 + lax.axis_index("xp")

    halves = [lax.ppermute(cut(hid_grad[0], h), "pipe", BACK) for h in range(2)]
    gathered = lax.all_gather(tokens, PLANE, axis=0)
    other = lax.ppermute(mine, "core", [(0, 1), (1, 0)])

    flat_expert = routes[0].reshape(-1)
    pairs = flat_expert.shape[0]
    number = jnp.arange(pairs, dtype=jnp.int32)
    earlier = (flat_expert[:, None] == flat_expert[None, :]) & (number[None, :] < number[:, None])
    slot = jnp.sum(earlier.astype(jnp.int32), axis=1)
    target = flat_expert * SLOTS + slot
    by_token = target.reshape(n_tokens, TOP)
    targets = exchange(jnp.broadcast_to(by_token.T[None], (DEVICES, TOP, n_tokens)))

    target, targets = after(target, targets)
    first = exchange(place(target, halves[0])).reshape(DEVICES * SHARE, hidden)
    lower = jnp.where(core == 0, mine, other)
    upper = jnp.where(core == 0, other, mine)
    target, lower, upper = after(target, lower, upper)
    second = exchange(place(target, halves[1])).reshape(DEVICES * SHARE, hidden)

    gathered, first = after(gathered, first)
    rows = pick(expert * SLOTS + core * SHARE, targets, gathered).reshape(DEVICES * SHARE, width)
    columns = width // COLUMN_PARTS
    slope_0 = after(derivative(bf16_dot(rows, lower, ((1,), (0,)))))
    early = terms([first], [slope_0], [lower], 0, width, dtype=jnp.float32)
    rows, early = after(rows, early)
    slope_1 = after(derivative(bf16_dot(rows, upper, ((1,), (0,)))))

    places = jnp.arange(EXPERTS * SLOTS, dtype=jnp.int32).reshape(EXPERTS, 1, SLOTS)
    places = jnp.broadcast_to(places, (EXPERTS, 2, SLOTS)).reshape(-1)
    hit = [by_token[:, k, None] == places[None, :] for k in range(TOP)]
    mix = sum(jnp.where(hit[k], probs[0][:, k, None], 0.0) for k in range(TOP))
    high = lax.reduce_precision(mix, 8, 7)
    mix = jnp.concatenate([high, mix - high]).astype(jnp.bfloat16)

    parts = []
    for j in range(COLUMN_PARTS):
        term = terms([second], [slope_1], [upper], j * columns, columns, base=early)
        returned = exchange(term.reshape(DEVICES, SHARE, columns)).reshape(-1, columns)
        both = bf16_dot(mix, returned, ((1,), (0,)))
        summed = (both[:n_tokens] + both[n_tokens:]).astype(jnp.bfloat16)
        parts.append(lax.ppermute(summed, "pipe", BACK))
    return jnp.concatenate(parts, axis=1)[None]


def solution(mesh):
    fine = Mesh(mesh.devices.reshape(4, 4, 2, 2, 2), ("pipe",) + PLANE)
    placed = (
        P("pipe", PLANE, None),
        P("pipe", PLANE, None, None),
        P("pipe", PLANE, None),
        P("pipe", PLANE, None),
        P("pipe", PLANE, None, None),
    )
    return jax.shard_map(
        local, mesh=fine, in_specs=placed, out_specs=P("pipe", PLANE, None), check_vma=False
    )
```

```python
import functools

import jax
import jax.numpy as jnp
from jax import lax
from jax.experimental import pallas as pl
from jax.experimental.pallas import tpu as pltpu
from jax.sharding import Mesh, PartitionSpec as P

EXPERTS = 8
TOP = 2
SLOTS = 64
PLANE = ("z", "xp", "p", "core")
DEVICES = 32
SHARE = SLOTS // 2
BACK = [((i + 1) % 4, i) for i in range(4)]
COLUMN_PARTS = 2
VMEM = 56 * 1024 * 1024


def exchange(block):
    return lax.all_to_all(block, PLANE, split_axis=0, concat_axis=0, tiled=True)


def after(*values):
    return lax.optimization_barrier(values if len(values) > 1 else values[0])


def derivative(gate_pre):
    squash = jax.nn.sigmoid(gate_pre)
    return (squash * (1.0 + gate_pre * (1.0 - squash))).astype(jnp.bfloat16)


def bf16_dot(a, b, dims):
    return lax.dot_general(a, b, (dims, ((), ())), preferred_element_type=jnp.float32)


def place_kernel(target_ref, grads_ref, out_ref):
    tokens, top, columns = grads_ref.shape
    places = lax.broadcasted_iota(jnp.int32, (EXPERTS * SLOTS, tokens * top), 0)
    hit = jnp.where(places == target_ref[...], 1.0, 0.0).astype(jnp.bfloat16)
    grads = grads_ref[...].reshape(tokens * top, columns)
    placed = jnp.dot(hit, grads, preferred_element_type=jnp.float32).astype(jnp.bfloat16)
    out_ref[:, 0] = placed.reshape(EXPERTS, 2, SHARE, columns)


def place(target, grads):
    tokens, top, width = grads.shape
    pairs, hidden = tokens * top, width // 2
    columns = 1024
    steps = hidden // columns
    out = pl.pallas_call(
        place_kernel,
        grid=(2, steps),
        in_specs=[
            pl.BlockSpec((1, pairs), lambda p, j: (0, 0)),
            pl.BlockSpec((tokens, top, columns), lambda p, j: (0, 0, p * steps + j)),
        ],
        out_specs=pl.BlockSpec((EXPERTS, 1, 2, SHARE, columns), lambda p, j: (0, p, 0, 0, j)),
        out_shape=jax.ShapeDtypeStruct((EXPERTS, 2, 2, SHARE, hidden), jnp.bfloat16),
        compiler_params=pltpu.CompilerParams(vmem_limit_bytes=VMEM),
        cost_estimate=pl.CostEstimate(
            flops=4 * EXPERTS * SLOTS * pairs * hidden,
            bytes_accessed=4 * (EXPERTS * SLOTS + pairs) * hidden,
            transcendentals=0,
        ),
        name="place_grads",
    )(target.reshape(1, pairs), grads)
    return out.reshape(DEVICES, SHARE, hidden)


SOURCES = 8


def pick_kernel(number_ref, tokens_ref, out_ref):
    n_tokens, width = tokens_ref.shape[1:]
    token = lax.broadcasted_iota(jnp.int32, (SHARE, n_tokens), 1) + 1
    nothing = jnp.zeros((SHARE, n_tokens), jnp.bfloat16)
    for i in range(0, SOURCES, 2):
        hits = [
            jnp.where(number_ref[i + n].astype(jnp.float32) == token.astype(jnp.float32), 1.0, 0.0)
            for n in range(2)
        ]
        hits = [hit.astype(jnp.bfloat16) for hit in hits]
        pair = jnp.concatenate(
            [
                jnp.concatenate([hits[0], nothing], axis=1),
                jnp.concatenate([nothing, hits[1]], axis=1),
            ],
            axis=0,
        )
        both = tokens_ref[i : i + 2].reshape(2 * n_tokens, width)
        rows = jnp.dot(pair, both, preferred_element_type=jnp.float32)
        out_ref[i : i + 2] = rows.astype(jnp.bfloat16).reshape(2, SHARE, width)


def pick(numbers, tokens):
    sources, n_tokens, width = tokens.shape
    return pl.pallas_call(
        pick_kernel,
        grid=(sources // SOURCES,),
        in_specs=[
            pl.BlockSpec((SOURCES, SHARE, n_tokens), lambda i: (i, 0, 0)),
            pl.BlockSpec((SOURCES, n_tokens, width), lambda i: (i, 0, 0)),
        ],
        out_specs=pl.BlockSpec((SOURCES, SHARE, width), lambda i: (i, 0, 0)),
        out_shape=jax.ShapeDtypeStruct((sources, SHARE, width), jnp.bfloat16),
        compiler_params=pltpu.CompilerParams(vmem_limit_bytes=VMEM),
        cost_estimate=pl.CostEstimate(
            flops=2 * sources * SHARE * n_tokens * width,
            bytes_accessed=2 * sources * (SHARE + n_tokens) * width,
            transcendentals=0,
        ),
        name="pick_rows",
    )(numbers, tokens)


def copy_kernel(in_ref, out_ref):
    out_ref[...] = in_ref[...]


def cut(grads, h):
    tokens, top, width = grads.shape
    columns = width // 8
    return pl.pallas_call(
        copy_kernel,
        grid=(2, 2),
        in_specs=[
            pl.BlockSpec((tokens, top, columns), lambda p, j: (0, 0, (2 * p + h) * 2 + j)),
        ],
        out_specs=pl.BlockSpec((tokens, top, columns), lambda p, j: (0, 0, 2 * p + j)),
        out_shape=jax.ShapeDtypeStruct((tokens, top, width // 2), grads.dtype),
        compiler_params=pltpu.CompilerParams(vmem_limit_bytes=VMEM),
        cost_estimate=pl.CostEstimate(
            flops=0, bytes_accessed=2 * tokens * top * width, transcendentals=0
        ),
        name="cut_grads",
    )(grads)


DEEP = 512
WIDE = 768


def term_kernel(n, based, *refs):
    grads, slopes, weights = refs[:n], refs[n : 2 * n], refs[2 * n : 3 * n]
    out_ref, gate, total = refs[-3:]
    j, k = pl.program_id(0), pl.program_id(1)

    @pl.when(j == 0)
    def _():
        for i in range(n):
            product = grads[i][...].astype(jnp.float32) * slopes[i][...].astype(jnp.float32)
            gate[n * k + i] = product.astype(jnp.bfloat16)

    def step():
        return sum(bf16_dot(gate[n * k + i], weights[i][...], ((1,), (1,))) for i in range(n))

    last = pl.num_programs(1) - 1

    @pl.when(k == 0)
    def _():
        total[...] = step() + refs[3 * n][...] if based else step()

    @pl.when((k > 0) & (k < last))
    def _():
        total[...] += step()

    @pl.when(k == last)
    def _():
        out_ref[...] = (total[...] + step()).astype(out_ref.dtype)


def terms(grads, slopes, weights, first, columns, base=None, dtype=jnp.bfloat16):
    n = len(grads)
    rows, hidden = grads[0].shape
    steps, offset, depth = columns // WIDE, first // WIDE, hidden // DEEP
    side = pl.BlockSpec((rows, DEEP), lambda j, k: (0, jnp.where(j == 0, k, depth - 1)))
    weight = pl.BlockSpec((WIDE, DEEP), lambda j, k: (offset + j, k))
    column = pl.BlockSpec((rows, WIDE), lambda j, k: (0, j))
    behind = pl.BlockSpec((rows, WIDE), lambda j, k: (0, offset + j))
    based = base is not None
    return pl.pallas_call(
        functools.partial(term_kernel, n, based),
        grid=(steps, depth),
        in_specs=[side] * (2 * n) + [weight] * n + [behind] * based,
        out_specs=column,
        out_shape=jax.ShapeDtypeStruct((rows, columns), dtype),
        scratch_shapes=[
            pltpu.VMEM((n * depth, rows, DEEP), jnp.bfloat16),
            pltpu.VMEM((rows, WIDE), jnp.float32),
        ],
        compiler_params=pltpu.CompilerParams(vmem_limit_bytes=VMEM),
        cost_estimate=pl.CostEstimate(
            flops=2 * n * rows * hidden * columns,
            bytes_accessed=2 * n * hidden * (2 * rows + columns) + 4 * rows * columns,
            transcendentals=0,
        ),
        name="terms",
    )(*grads, *slopes, *weights, *([base] if based else []))


def local(acts, hid_grad, routes, probs, w_gate):
    tokens = acts[0]
    n_tokens, width = tokens.shape
    mine = w_gate[0, 0]
    hidden = mine.shape[1]
    core = lax.axis_index("core")
    rows_here = DEVICES * SHARE

    sent_width = width // 2
    gathered = lax.all_gather(tokens[:, sent_width:], PLANE, axis=0)

    flat_expert = routes[0].reshape(-1)
    pairs = flat_expert.shape[0]
    number = jnp.arange(pairs, dtype=jnp.int32)
    earlier = (flat_expert[:, None] == flat_expert[None, :]) & (number[None, :] < number[:, None])
    slot = jnp.sum(earlier.astype(jnp.int32), axis=1)
    target = flat_expert * SLOTS + slot
    by_token = target.reshape(n_tokens, TOP)

    places = jnp.arange(EXPERTS * SLOTS, dtype=jnp.int32).reshape(EXPERTS, 1, SLOTS)
    places = jnp.broadcast_to(places, (EXPERTS, 2, SLOTS)).reshape(-1)
    row_hit = [places[:, None] == by_token[None, :, k] for k in range(TOP)]
    place_token = (row_hit[0] | row_hit[1]).astype(jnp.bfloat16)
    numbered = jnp.broadcast_to(
        jnp.arange(1, n_tokens + 1, dtype=jnp.int32)[:, None], (n_tokens, n_tokens)
    ).astype(jnp.bfloat16)
    sent = jnp.concatenate([tokens[:, :sent_width], numbered], axis=1)
    sent = bf16_dot(place_token, sent, ((1,), (0,))).astype(jnp.bfloat16)
    got = exchange(sent.reshape(DEVICES, SHARE, sent_width + n_tokens))
    rows_0 = got[:, :, :sent_width].reshape(rows_here, sent_width)
    numbers = got[:, :, sent_width:]

    pieces = [cut(hid_grad[0], h) for h in range(2)]
    halves = [lax.ppermute(piece, "pipe", BACK) for piece in pieces]
    other = lax.ppermute(mine, "core", [(0, 1), (1, 0)])
    lower = jnp.where(core == 0, mine, other)
    upper = jnp.where(core == 0, other, mine)

    first = exchange(place(target, halves[0])).reshape(rows_here, hidden)
    below = [
        after(bf16_dot(rows_0, w[:sent_width], ((1,), (0,)))) for w in (lower, upper)
    ]
    target, below[0], below[1] = after(target, below[0], below[1])
    second = exchange(place(target, halves[1])).reshape(rows_here, hidden)

    rows_1 = pick(numbers, gathered).reshape(rows_here, width - sent_width)
    slope_0 = after(derivative(below[0] + bf16_dot(rows_1, lower[sent_width:], ((1,), (0,)))))
    early = terms([first], [slope_0], [lower], 0, width, dtype=jnp.float32)
    rows_1, early = after(rows_1, early)
    slope_1 = after(derivative(below[1] + bf16_dot(rows_1, upper[sent_width:], ((1,), (0,)))))

    columns = width // COLUMN_PARTS
    hit = [by_token[:, k, None] == places[None, :] for k in range(TOP)]
    mix = sum(jnp.where(hit[k], probs[0][:, k, None], 0.0) for k in range(TOP))
    high = lax.reduce_precision(mix, 8, 7)
    mix = jnp.concatenate([high, mix - high]).astype(jnp.bfloat16)

    parts = []
    for j in range(COLUMN_PARTS):
        term = terms([second], [slope_1], [upper], j * columns, columns, base=early)
        returned = exchange(term.reshape(DEVICES, SHARE, columns)).reshape(-1, columns)
        both = bf16_dot(mix, returned, ((1,), (0,)))
        summed = (both[:n_tokens] + both[n_tokens:]).astype(jnp.bfloat16)
        parts.append(lax.ppermute(summed, "pipe", BACK))
    return jnp.concatenate(parts, axis=1)[None]


def solution(mesh):
    fine = Mesh(mesh.devices.reshape(4, 4, 2, 2, 2), ("pipe",) + PLANE)
    placed = (
        P("pipe", PLANE, None),
        P("pipe", PLANE, None, None),
        P("pipe", PLANE, None),
        P("pipe", PLANE, None),
        P("pipe", PLANE, None, None),
    )
    return jax.shard_map(
        local, mesh=fine, in_specs=placed, out_specs=P("pipe", PLANE, None), check_vma=False
    )
```

```python
import jax
import jax.numpy as jnp
from jax import lax
from jax.experimental import pallas as pl
from jax.experimental.pallas import tpu as pltpu
from jax.sharding import Mesh, PartitionSpec as P

EXPERTS = 8
TOP = 2
SLOTS = 64
PLANE = ("z", "xp", "p", "core")
DEVICES = 32
SHARE = SLOTS // 2
BACK = [((i + 1) % 4, i) for i in range(4)]
COLUMN_PARTS = 2
VMEM = 56 * 1024 * 1024


def exchange(block):
    return lax.all_to_all(block, PLANE, split_axis=0, concat_axis=0, tiled=True)


def after(*values):
    return lax.optimization_barrier(values if len(values) > 1 else values[0])


def derivative(gate_pre):
    squash = jax.nn.sigmoid(gate_pre)
    return (squash * (1.0 + gate_pre * (1.0 - squash))).astype(jnp.bfloat16)


def bf16_dot(a, b, dims):
    return lax.dot_general(a, b, (dims, ((), ())), preferred_element_type=jnp.float32)


def place_kernel(target_ref, grads_ref, out_ref):
    tokens, top, columns = grads_ref.shape
    places = lax.broadcasted_iota(jnp.int32, (EXPERTS * SLOTS, tokens * top), 0)
    hit = jnp.where(places == target_ref[...], 1.0, 0.0).astype(jnp.bfloat16)
    grads = grads_ref[...].reshape(tokens * top, columns)
    placed = jnp.dot(hit, grads, preferred_element_type=jnp.float32).astype(jnp.bfloat16)
    out_ref[:, 0] = placed.reshape(EXPERTS, 2, SHARE, columns)


def place(target, grads):
    tokens, top, width = grads.shape
    pairs, hidden = tokens * top, width // 2
    columns = 1024
    steps = hidden // columns
    out = pl.pallas_call(
        place_kernel,
        grid=(2, steps),
        in_specs=[
            pl.BlockSpec((1, pairs), lambda p, j: (0, 0)),
            pl.BlockSpec((tokens, top, columns), lambda p, j: (0, 0, p * steps + j)),
        ],
        out_specs=pl.BlockSpec((EXPERTS, 1, 2, SHARE, columns), lambda p, j: (0, p, 0, 0, j)),
        out_shape=jax.ShapeDtypeStruct((EXPERTS, 2, 2, SHARE, hidden), jnp.bfloat16),
        compiler_params=pltpu.CompilerParams(vmem_limit_bytes=VMEM),
        cost_estimate=pl.CostEstimate(
            flops=4 * EXPERTS * SLOTS * pairs * hidden,
            bytes_accessed=4 * (EXPERTS * SLOTS + pairs) * hidden,
            transcendentals=0,
        ),
        name="place_grads",
    )(target.reshape(1, pairs), grads)
    return out.reshape(DEVICES, SHARE, hidden)


SOURCES = 8


def pick_kernel(number_ref, tokens_ref, out_ref):
    n_tokens, width = tokens_ref.shape[1:]
    token = lax.broadcasted_iota(jnp.int32, (SHARE, n_tokens), 1) + 1
    nothing = jnp.zeros((SHARE, n_tokens), jnp.bfloat16)
    for i in range(0, SOURCES, 2):
        hits = [
            jnp.where(number_ref[i + n].astype(jnp.float32) == token.astype(jnp.float32), 1.0, 0.0)
            for n in range(2)
        ]
        hits = [hit.astype(jnp.bfloat16) for hit in hits]
        pair = jnp.concatenate(
            [
                jnp.concatenate([hits[0], nothing], axis=1),
                jnp.concatenate([nothing, hits[1]], axis=1),
            ],
            axis=0,
        )
        both = tokens_ref[i : i + 2].reshape(2 * n_tokens, width)
        rows = jnp.dot(pair, both, preferred_element_type=jnp.float32)
        out_ref[i : i + 2] = rows.astype(jnp.bfloat16).reshape(2, SHARE, width)


def pick(numbers, tokens):
    sources, n_tokens, width = tokens.shape
    return pl.pallas_call(
        pick_kernel,
        grid=(sources // SOURCES,),
        in_specs=[
            pl.BlockSpec((SOURCES, SHARE, n_tokens), lambda i: (i, 0, 0)),
            pl.BlockSpec((SOURCES, n_tokens, width), lambda i: (i, 0, 0)),
        ],
        out_specs=pl.BlockSpec((SOURCES, SHARE, width), lambda i: (i, 0, 0)),
        out_shape=jax.ShapeDtypeStruct((sources, SHARE, width), jnp.bfloat16),
        compiler_params=pltpu.CompilerParams(vmem_limit_bytes=VMEM),
        cost_estimate=pl.CostEstimate(
            flops=2 * sources * SHARE * n_tokens * width,
            bytes_accessed=2 * sources * (SHARE + n_tokens) * width,
            transcendentals=0,
        ),
        name="pick_rows",
    )(numbers, tokens)


def copy_kernel(in_ref, out_ref):
    out_ref[...] = in_ref[...]


def cut(grads, h):
    tokens, top, width = grads.shape
    columns = width // 8
    return pl.pallas_call(
        copy_kernel,
        grid=(2, 2),
        in_specs=[
            pl.BlockSpec((tokens, top, columns), lambda p, j: (0, 0, (2 * p + h) * 2 + j)),
        ],
        out_specs=pl.BlockSpec((tokens, top, columns), lambda p, j: (0, 0, 2 * p + j)),
        out_shape=jax.ShapeDtypeStruct((tokens, top, width // 2), grads.dtype),
        compiler_params=pltpu.CompilerParams(vmem_limit_bytes=VMEM),
        cost_estimate=pl.CostEstimate(
            flops=0, bytes_accessed=2 * tokens * top * width, transcendentals=0
        ),
        name="cut_grads",
    )(grads)


def products(grads, slopes):
    return (grads.astype(jnp.float32) * slopes.astype(jnp.float32)).astype(jnp.bfloat16)


def local(acts, hid_grad, routes, probs, w_gate):
    tokens = acts[0]
    n_tokens, width = tokens.shape
    mine = w_gate[0, 0]
    hidden = mine.shape[1]
    core = lax.axis_index("core")
    rows_here = DEVICES * SHARE

    sent_width = width // 2
    gathered = lax.all_gather(tokens[:, sent_width:], PLANE, axis=0)

    flat_expert = routes[0].reshape(-1)
    pairs = flat_expert.shape[0]
    number = jnp.arange(pairs, dtype=jnp.int32)
    earlier = (flat_expert[:, None] == flat_expert[None, :]) & (number[None, :] < number[:, None])
    slot = jnp.sum(earlier.astype(jnp.int32), axis=1)
    target = flat_expert * SLOTS + slot
    by_token = target.reshape(n_tokens, TOP)

    places = jnp.arange(EXPERTS * SLOTS, dtype=jnp.int32).reshape(EXPERTS, 1, SLOTS)
    places = jnp.broadcast_to(places, (EXPERTS, 2, SLOTS)).reshape(-1)
    row_hit = [places[:, None] == by_token[None, :, k] for k in range(TOP)]
    place_token = (row_hit[0] | row_hit[1]).astype(jnp.bfloat16)
    numbered = jnp.broadcast_to(
        jnp.arange(1, n_tokens + 1, dtype=jnp.int32)[:, None], (n_tokens, n_tokens)
    ).astype(jnp.bfloat16)
    sent = jnp.concatenate([tokens[:, :sent_width], numbered], axis=1)
    sent = bf16_dot(place_token, sent, ((1,), (0,))).astype(jnp.bfloat16)
    got = exchange(sent.reshape(DEVICES, SHARE, sent_width + n_tokens))
    rows_0 = got[:, :, :sent_width].reshape(rows_here, sent_width)
    numbers = got[:, :, sent_width:]

    pieces = [cut(hid_grad[0], h) for h in range(2)]
    halves = [lax.ppermute(piece, "pipe", BACK) for piece in pieces]
    other = lax.ppermute(mine, "core", [(0, 1), (1, 0)])
    lower = jnp.where(core == 0, mine, other)
    upper = jnp.where(core == 0, other, mine)

    first = exchange(place(target, halves[0])).reshape(rows_here, hidden)
    below = [
        after(bf16_dot(rows_0, w[:sent_width], ((1,), (0,)))) for w in (lower, upper)
    ]
    target, below[0], below[1] = after(target, below[0], below[1])
    second = exchange(place(target, halves[1])).reshape(rows_here, hidden)

    gathered, first = after(gathered, first)
    rows_1 = pick(numbers, gathered).reshape(rows_here, width - sent_width)
    slope_0 = after(derivative(below[0] + bf16_dot(rows_1, lower[sent_width:], ((1,), (0,)))))
    columns = width // COLUMN_PARTS
    early = []
    for j in range(COLUMN_PARTS):
        part = lower[j * columns : (j + 1) * columns]
        early.append(after(bf16_dot(products(*after(first, slope_0)), part, ((1,), (1,)))))
    rows_1, early[0], early[1] = after(rows_1, *early)
    slope_1 = after(derivative(below[1] + bf16_dot(rows_1, upper[sent_width:], ((1,), (0,)))))

    hit = [by_token[:, k, None] == places[None, :] for k in range(TOP)]
    mix = sum(jnp.where(hit[k], probs[0][:, k, None], 0.0) for k in range(TOP))
    high = lax.reduce_precision(mix, 8, 7)
    mix = jnp.concatenate([high, mix - high]).astype(jnp.bfloat16)

    parts = []
    for j in range(COLUMN_PARTS):
        part = upper[j * columns : (j + 1) * columns]
        late = bf16_dot(products(*after(second, slope_1)), part, ((1,), (1,)))
        term = (early[j] + late).astype(jnp.bfloat16)
        returned = exchange(term.reshape(DEVICES, SHARE, columns)).reshape(-1, columns)
        both = bf16_dot(mix, returned, ((1,), (0,)))
        summed = (both[:n_tokens] + both[n_tokens:]).astype(jnp.bfloat16)
        parts.append(lax.ppermute(summed, "pipe", BACK))
    return jnp.concatenate(parts, axis=1)[None]


def solution(mesh):
    fine = Mesh(mesh.devices.reshape(4, 4, 2, 2, 2), ("pipe",) + PLANE)
    placed = (
        P("pipe", PLANE, None),
        P("pipe", PLANE, None, None),
        P("pipe", PLANE, None),
        P("pipe", PLANE, None),
        P("pipe", PLANE, None, None),
    )
    return jax.shard_map(
        local, mesh=fine, in_specs=placed, out_specs=P("pipe", PLANE, None), check_vma=False
    )
```

```python
import functools

import jax
import jax.numpy as jnp
from jax import lax
from jax.experimental import pallas as pl
from jax.experimental.pallas import tpu as pltpu
from jax.sharding import Mesh, PartitionSpec as P

EXPERTS = 8
TOP = 2
SLOTS = 64
PLANE = ("z", "xp", "p", "core")
DEVICES = 32
SHARE = SLOTS // 2
BACK = [((i + 1) % 4, i) for i in range(4)]
COLUMN_PARTS = 2
SHARDS = 4
FIRST = 1536
VMEM = 56 * 1024 * 1024


def exchange(block):
    return lax.all_to_all(block, PLANE, split_axis=0, concat_axis=0, tiled=True)


def after(*values):
    return lax.optimization_barrier(values if len(values) > 1 else values[0])


def derivative(gate_pre):
    squash = jax.nn.sigmoid(gate_pre)
    return (squash * (1.0 + gate_pre * (1.0 - squash))).astype(jnp.bfloat16)


def bf16_dot(a, b, dims):
    return lax.dot_general(a, b, (dims, ((), ())), preferred_element_type=jnp.float32)


def place_kernel(target_ref, grads_ref, out_ref):
    tokens, top, columns = grads_ref.shape
    places = lax.broadcasted_iota(jnp.int32, (EXPERTS * SLOTS, tokens * top), 0)
    hit = jnp.where(places == target_ref[...], 1.0, 0.0).astype(jnp.bfloat16)
    grads = grads_ref[...].reshape(tokens * top, columns)
    placed = jnp.dot(hit, grads, preferred_element_type=jnp.float32).astype(jnp.bfloat16)
    out_ref[:, 0] = placed.reshape(EXPERTS, 2, SHARE, columns)


def place(target, grads):
    tokens, top, width = grads.shape
    pairs, hidden = tokens * top, width // 2
    columns = 1024
    steps = hidden // columns
    out = pl.pallas_call(
        place_kernel,
        grid=(2, steps),
        in_specs=[
            pl.BlockSpec((1, pairs), lambda p, j: (0, 0)),
            pl.BlockSpec((tokens, top, columns), lambda p, j: (0, 0, p * steps + j)),
        ],
        out_specs=pl.BlockSpec((EXPERTS, 1, 2, SHARE, columns), lambda p, j: (0, p, 0, 0, j)),
        out_shape=jax.ShapeDtypeStruct((EXPERTS, 2, 2, SHARE, hidden), jnp.bfloat16),
        compiler_params=pltpu.CompilerParams(vmem_limit_bytes=VMEM),
        cost_estimate=pl.CostEstimate(
            flops=4 * EXPERTS * SLOTS * pairs * hidden,
            bytes_accessed=4 * (EXPERTS * SLOTS + pairs) * hidden,
            transcendentals=0,
        ),
        name="place_grads",
    )(target.reshape(1, pairs), grads)
    return out.reshape(DEVICES, SHARE, hidden)


def cut_kernel(shards, start, size, in_ref, out_ref, sems):
    hidden = in_ref.shape[2] // shards
    copies = [
        pltpu.make_async_copy(
            in_ref.at[:, :, pl.ds(f * hidden + start, size)],
            out_ref.at[:, :, pl.ds(f * size, size)],
            sems.at[f],
        )
        for f in range(shards)
    ]
    for copy in copies:
        copy.start()
    for copy in copies:
        copy.wait()


def cut(grads, shards, start, size):
    tokens, top, _ = grads.shape
    return pl.pallas_call(
        functools.partial(cut_kernel, shards, start, size),
        in_specs=[pl.BlockSpec(memory_space=pl.ANY)],
        out_specs=pl.BlockSpec(memory_space=pl.ANY),
        out_shape=jax.ShapeDtypeStruct((tokens, top, shards * size), grads.dtype),
        scratch_shapes=[pltpu.SemaphoreType.DMA((shards,))],
        cost_estimate=pl.CostEstimate(
            flops=0, bytes_accessed=4 * tokens * top * shards * size, transcendentals=0
        ),
        name="cut_grads",
    )(grads)


def products(grads, slopes):
    return (grads.astype(jnp.float32) * slopes.astype(jnp.float32)).astype(jnp.bfloat16)


def local(acts, hid_grad, routes, probs, w_gate):
    tokens = acts[0]
    n_tokens, width = tokens.shape
    mine = w_gate[0, 0]
    hidden = mine.shape[1]
    core = lax.axis_index("core")
    rows_here = DEVICES * SHARE

    flat_expert = routes[0].reshape(-1)
    pairs = flat_expert.shape[0]
    number = jnp.arange(pairs, dtype=jnp.int32)
    earlier = (flat_expert[:, None] == flat_expert[None, :]) & (number[None, :] < number[:, None])
    slot = jnp.sum(earlier.astype(jnp.int32), axis=1)
    target = flat_expert * SLOTS + slot
    by_token = target.reshape(n_tokens, TOP)

    places = jnp.arange(EXPERTS * SLOTS, dtype=jnp.int32).reshape(EXPERTS, 1, SLOTS)
    places = jnp.broadcast_to(places, (EXPERTS, 2, SLOTS)).reshape(-1)
    row_hit = [places[:, None] == by_token[None, :, k] for k in range(TOP)]
    place_token = (row_hit[0] | row_hit[1]).astype(jnp.bfloat16)
    sent = bf16_dot(place_token, tokens, ((1,), (0,))).astype(jnp.bfloat16)
    rows = exchange(sent.reshape(DEVICES, SHARE, width)).reshape(rows_here, width)

    shares = ((0, FIRST), (FIRST, hidden - FIRST))
    pieces = [cut(hid_grad[0], SHARDS, *share) for share in shares]
    parts = [lax.ppermute(piece, "pipe", BACK) for piece in pieces]
    other = lax.ppermute(mine, "core", [(0, 1), (1, 0)])
    shard = (jnp.where(core == 0, mine, other), jnp.where(core == 0, other, mine))
    weights = [
        jnp.concatenate([w[:, start : start + size] for w in shard], axis=1)
        for start, size in shares
    ]
    weights = list(after(*weights))

    placed = place(target, parts[0])
    first = exchange(placed).reshape(rows_here, 2 * FIRST)
    slopes = [after(derivative(bf16_dot(rows, w, ((1,), (0,))))) for w in weights]
    target, *slopes = after(target, *slopes)
    second = exchange(place(target, parts[1])).reshape(rows_here, 2 * (hidden - FIRST))

    columns = width // COLUMN_PARTS
    early = []
    for j in range(COLUMN_PARTS):
        part = weights[0][j * columns : (j + 1) * columns]
        early.append(after(bf16_dot(products(*after(first, slopes[0])), part, ((1,), (1,)))))
    hit = [by_token[:, k, None] == places[None, :] for k in range(TOP)]
    mix = sum(jnp.where(hit[k], probs[0][:, k, None], 0.0) for k in range(TOP))
    high = lax.reduce_precision(mix, 8, 7)
    mix = jnp.concatenate([high, mix - high]).astype(jnp.bfloat16)

    outs = []
    for j in range(COLUMN_PARTS):
        part = weights[1][j * columns : (j + 1) * columns]
        late = bf16_dot(products(*after(second, slopes[1])), part, ((1,), (1,)))
        term = (early[j] + late).astype(jnp.bfloat16)
        returned = exchange(term.reshape(DEVICES, SHARE, columns)).reshape(-1, columns)
        both = bf16_dot(mix, returned, ((1,), (0,)))
        summed = (both[:n_tokens] + both[n_tokens:]).astype(jnp.bfloat16)
        outs.append(lax.ppermute(summed, "pipe", BACK))
    return jnp.concatenate(outs, axis=1)[None]


def solution(mesh):
    fine = Mesh(mesh.devices.reshape(4, 4, 2, 2, 2), ("pipe",) + PLANE)
    placed = (
        P("pipe", PLANE, None),
        P("pipe", PLANE, None, None),
        P("pipe", PLANE, None),
        P("pipe", PLANE, None),
        P("pipe", PLANE, None, None),
    )
    return jax.shard_map(
        local, mesh=fine, in_specs=placed, out_specs=P("pipe", PLANE, None), check_vma=False
    )
```

```python
import jax
import jax.numpy as jnp
from jax import lax
from jax.experimental import pallas as pl
from jax.experimental.pallas import tpu as pltpu
from jax.sharding import Mesh, PartitionSpec as P

EXPERTS = 8
TOP = 2
SLOTS = 64
PLANE = ("z", "xp", "p", "core")
DEVICES = 32
SHARE = SLOTS // 2
BACK = [((i + 1) % 4, i) for i in range(4)]
COLUMN_PARTS = 2
VMEM = 56 * 1024 * 1024


def exchange(block):
    return lax.all_to_all(block, PLANE, split_axis=0, concat_axis=0, tiled=True)


def after(*values):
    return lax.optimization_barrier(values if len(values) > 1 else values[0])


def derivative(gate_pre):
    squash = jax.nn.sigmoid(gate_pre)
    return (squash * (1.0 + gate_pre * (1.0 - squash))).astype(jnp.bfloat16)


def bf16_dot(a, b, dims):
    return lax.dot_general(a, b, (dims, ((), ())), preferred_element_type=jnp.float32)


def place_kernel(target_ref, grads_ref, out_ref):
    tokens, top, columns = grads_ref.shape
    places = lax.broadcasted_iota(jnp.int32, (EXPERTS * SLOTS, tokens * top), 0)
    hit = jnp.where(places == target_ref[...], 1.0, 0.0).astype(jnp.bfloat16)
    grads = grads_ref[...].reshape(tokens * top, columns)
    placed = jnp.dot(hit, grads, preferred_element_type=jnp.float32).astype(jnp.bfloat16)
    out_ref[:, 0] = placed.reshape(EXPERTS, 2, SHARE, columns)


def place(target, grads):
    tokens, top, width = grads.shape
    pairs, hidden = tokens * top, width // 2
    columns = hidden
    steps = 1
    out = pl.pallas_call(
        place_kernel,
        grid=(2, steps),
        in_specs=[
            pl.BlockSpec((1, pairs), lambda p, j: (0, 0)),
            pl.BlockSpec((tokens, top, columns), lambda p, j: (0, 0, p * steps + j)),
        ],
        out_specs=pl.BlockSpec((EXPERTS, 1, 2, SHARE, columns), lambda p, j: (0, p, 0, 0, j)),
        out_shape=jax.ShapeDtypeStruct((EXPERTS, 2, 2, SHARE, hidden), jnp.bfloat16),
        compiler_params=pltpu.CompilerParams(vmem_limit_bytes=VMEM),
        cost_estimate=pl.CostEstimate(
            flops=4 * EXPERTS * SLOTS * pairs * hidden,
            bytes_accessed=4 * (EXPERTS * SLOTS + pairs) * hidden,
            transcendentals=0,
        ),
        name="place_grads",
    )(target.reshape(1, pairs), grads)
    return out.reshape(DEVICES, SHARE, hidden)


SOURCES = 8


def pick_kernel(number_ref, tokens_ref, out_ref):
    n_tokens, width = tokens_ref.shape[1:]
    token = lax.broadcasted_iota(jnp.int32, (SHARE, n_tokens), 1) + 1
    nothing = jnp.zeros((SHARE, n_tokens), jnp.bfloat16)
    for i in range(0, SOURCES, 2):
        hits = [
            jnp.where(number_ref[i + n].astype(jnp.float32) == token.astype(jnp.float32), 1.0, 0.0)
            for n in range(2)
        ]
        hits = [hit.astype(jnp.bfloat16) for hit in hits]
        pair = jnp.concatenate(
            [
                jnp.concatenate([hits[0], nothing], axis=1),
                jnp.concatenate([nothing, hits[1]], axis=1),
            ],
            axis=0,
        )
        both = tokens_ref[i : i + 2].reshape(2 * n_tokens, width)
        rows = jnp.dot(pair, both, preferred_element_type=jnp.float32)
        out_ref[i : i + 2] = rows.astype(jnp.bfloat16).reshape(2, SHARE, width)


def pick(numbers, tokens):
    sources, n_tokens, width = tokens.shape
    return pl.pallas_call(
        pick_kernel,
        grid=(sources // SOURCES,),
        in_specs=[
            pl.BlockSpec((SOURCES, SHARE, n_tokens), lambda i: (i, 0, 0)),
            pl.BlockSpec((SOURCES, n_tokens, width), lambda i: (i, 0, 0)),
        ],
        out_specs=pl.BlockSpec((SOURCES, SHARE, width), lambda i: (i, 0, 0)),
        out_shape=jax.ShapeDtypeStruct((sources, SHARE, width), jnp.bfloat16),
        compiler_params=pltpu.CompilerParams(vmem_limit_bytes=VMEM),
        cost_estimate=pl.CostEstimate(
            flops=2 * sources * SHARE * n_tokens * width,
            bytes_accessed=2 * sources * (SHARE + n_tokens) * width,
            transcendentals=0,
        ),
        name="pick_rows",
    )(numbers, tokens)


def copy_kernel(in_ref, out_ref):
    out_ref[...] = in_ref[...]


def cut(grads, h):
    tokens, top, width = grads.shape
    columns = width // 4
    return pl.pallas_call(
        copy_kernel,
        grid=(2,),
        in_specs=[pl.BlockSpec((tokens, top, columns), lambda p: (0, 0, 2 * p + h))],
        out_specs=pl.BlockSpec((tokens, top, columns), lambda p: (0, 0, p)),
        out_shape=jax.ShapeDtypeStruct((tokens, top, width // 2), grads.dtype),
        compiler_params=pltpu.CompilerParams(vmem_limit_bytes=VMEM),
        cost_estimate=pl.CostEstimate(
            flops=0, bytes_accessed=2 * tokens * top * width, transcendentals=0
        ),
        name="cut_grads",
    )(grads)


def products(grads, slopes):
    return (grads.astype(jnp.float32) * slopes.astype(jnp.float32)).astype(jnp.bfloat16)


def local(acts, hid_grad, routes, probs, w_gate):
    tokens = acts[0]
    n_tokens, width = tokens.shape
    mine = w_gate[0, 0]
    hidden = mine.shape[1]
    core = lax.axis_index("core")
    rows_here = DEVICES * SHARE

    sent_width = width // 2
    gathered = lax.all_gather(tokens[:, sent_width:], PLANE, axis=0)

    flat_expert = routes[0].reshape(-1)
    pairs = flat_expert.shape[0]
    number = jnp.arange(pairs, dtype=jnp.int32)
    earlier = (flat_expert[:, None] == flat_expert[None, :]) & (number[None, :] < number[:, None])
    slot = jnp.sum(earlier.astype(jnp.int32), axis=1)
    target = flat_expert * SLOTS + slot
    by_token = target.reshape(n_tokens, TOP)

    places = jnp.arange(EXPERTS * SLOTS, dtype=jnp.int32).reshape(EXPERTS, 1, SLOTS)
    places = jnp.broadcast_to(places, (EXPERTS, 2, SLOTS)).reshape(-1)
    row_hit = [places[:, None] == by_token[None, :, k] for k in range(TOP)]
    place_token = (row_hit[0] | row_hit[1]).astype(jnp.bfloat16)
    numbered = jnp.broadcast_to(
        jnp.arange(1, n_tokens + 1, dtype=jnp.int32)[:, None], (n_tokens, n_tokens)
    ).astype(jnp.bfloat16)
    sent = jnp.concatenate([tokens[:, :sent_width], numbered], axis=1)
    sent = bf16_dot(place_token, sent, ((1,), (0,))).astype(jnp.bfloat16)
    got = exchange(sent.reshape(DEVICES, SHARE, sent_width + n_tokens))
    rows_0 = got[:, :, :sent_width].reshape(rows_here, sent_width)
    numbers = got[:, :, sent_width:]

    pieces = [cut(hid_grad[0], h) for h in range(2)]
    halves = [lax.ppermute(piece, "pipe", BACK) for piece in pieces]
    other = lax.ppermute(mine, "core", [(0, 1), (1, 0)])
    lower = jnp.where(core == 0, mine, other)
    upper = jnp.where(core == 0, other, mine)

    first = exchange(place(target, halves[0])).reshape(rows_here, hidden)
    below = [
        after(bf16_dot(rows_0, w[:sent_width], ((1,), (0,)))) for w in (lower, upper)
    ]
    target, below[0], below[1] = after(target, below[0], below[1])
    second = exchange(place(target, halves[1])).reshape(rows_here, hidden)

    gathered, first = after(gathered, first)
    rows_1 = pick(numbers, gathered).reshape(rows_here, width - sent_width)
    slope_0 = after(derivative(below[0] + bf16_dot(rows_1, lower[sent_width:], ((1,), (0,)))))
    columns = width // COLUMN_PARTS
    early = []
    for j in range(COLUMN_PARTS):
        part = lower[j * columns : (j + 1) * columns]
        term = bf16_dot(products(*after(first, slope_0)), part, ((1,), (1,)))
        early.append(after(term.astype(jnp.bfloat16)))
    rows_1, early[0], early[1] = after(rows_1, *early)
    slope_1 = after(derivative(below[1] + bf16_dot(rows_1, upper[sent_width:], ((1,), (0,)))))

    hit = [by_token[:, k, None] == places[None, :] for k in range(TOP)]
    mix = sum(jnp.where(hit[k], probs[0][:, k, None], 0.0) for k in range(TOP))
    high = lax.reduce_precision(mix, 8, 7)
    mix = jnp.concatenate([high, mix - high]).astype(jnp.bfloat16)

    parts = []
    for j in range(COLUMN_PARTS):
        part = upper[j * columns : (j + 1) * columns]
        late = bf16_dot(products(*after(second, slope_1)), part, ((1,), (1,)))
        term = (early[j].astype(jnp.float32) + late).astype(jnp.bfloat16)
        returned = exchange(term.reshape(DEVICES, SHARE, columns)).reshape(-1, columns)
        both = bf16_dot(mix, returned, ((1,), (0,)))
        summed = (both[:n_tokens] + both[n_tokens:]).astype(jnp.bfloat16)
        parts.append(lax.ppermute(summed, "pipe", BACK))
    return jnp.concatenate(parts, axis=1)[None]


def solution(mesh):
    fine = Mesh(mesh.devices.reshape(4, 4, 2, 2, 2), ("pipe",) + PLANE)
    placed = (
        P("pipe", PLANE, None),
        P("pipe", PLANE, None, None),
        P("pipe", PLANE, None),
        P("pipe", PLANE, None),
        P("pipe", PLANE, None, None),
    )
    return jax.shard_map(
        local, mesh=fine, in_specs=placed, out_specs=P("pipe", PLANE, None), check_vma=False
    )
```

```python
import jax
import jax.numpy as jnp
from jax import lax
from jax.experimental import pallas as pl
from jax.experimental.pallas import tpu as pltpu
from jax.sharding import Mesh, PartitionSpec as P

EXPERTS = 8
TOP = 2
SLOTS = 64
PLANE = ("z", "xp", "p", "core")
DEVICES = 32
SHARE = SLOTS // 2
BACK = [((i + 1) % 4, i) for i in range(4)]
COLUMN_PARTS = 2
VMEM = 56 * 1024 * 1024


def exchange(block):
    return lax.all_to_all(block, PLANE, split_axis=0, concat_axis=0, tiled=True)


def after(*values):
    return lax.optimization_barrier(values if len(values) > 1 else values[0])


def derivative(gate_pre):
    squash = jax.nn.sigmoid(gate_pre)
    return (squash * (1.0 + gate_pre * (1.0 - squash))).astype(jnp.bfloat16)


def bf16_dot(a, b, dims):
    return lax.dot_general(a, b, (dims, ((), ())), preferred_element_type=jnp.float32)


def place_kernel(target_ref, grads_ref, out_ref):
    tokens, top, columns = grads_ref.shape
    places = lax.broadcasted_iota(jnp.int32, (EXPERTS * SLOTS, tokens * top), 0)
    hit = jnp.where(places == target_ref[...], 1.0, 0.0).astype(jnp.bfloat16)
    grads = grads_ref[...].reshape(tokens * top, columns)
    placed = jnp.dot(hit, grads, preferred_element_type=jnp.float32).astype(jnp.bfloat16)
    out_ref[:, 0] = placed.reshape(EXPERTS, 2, SHARE, columns)


def place(target, grads):
    tokens, top, width = grads.shape
    pairs, hidden = tokens * top, width // 2
    columns = hidden
    steps = 1
    out = pl.pallas_call(
        place_kernel,
        grid=(2, steps),
        in_specs=[
            pl.BlockSpec((1, pairs), lambda p, j: (0, 0)),
            pl.BlockSpec((tokens, top, columns), lambda p, j: (0, 0, p * steps + j)),
        ],
        out_specs=pl.BlockSpec((EXPERTS, 1, 2, SHARE, columns), lambda p, j: (0, p, 0, 0, j)),
        out_shape=jax.ShapeDtypeStruct((EXPERTS, 2, 2, SHARE, hidden), jnp.bfloat16),
        compiler_params=pltpu.CompilerParams(vmem_limit_bytes=VMEM),
        cost_estimate=pl.CostEstimate(
            flops=4 * EXPERTS * SLOTS * pairs * hidden,
            bytes_accessed=4 * (EXPERTS * SLOTS + pairs) * hidden,
            transcendentals=0,
        ),
        name="place_grads",
    )(target.reshape(1, pairs), grads)
    return out.reshape(DEVICES, SHARE, hidden)


def copy_kernel(in_ref, out_ref):
    out_ref[...] = in_ref[...]


def cut(grads, h):
    tokens, top, width = grads.shape
    columns = width // 4
    return pl.pallas_call(
        copy_kernel,
        grid=(2,),
        in_specs=[pl.BlockSpec((tokens, top, columns), lambda p: (0, 0, 2 * p + h))],
        out_specs=pl.BlockSpec((tokens, top, columns), lambda p: (0, 0, p)),
        out_shape=jax.ShapeDtypeStruct((tokens, top, width // 2), grads.dtype),
        compiler_params=pltpu.CompilerParams(vmem_limit_bytes=VMEM),
        cost_estimate=pl.CostEstimate(
            flops=0, bytes_accessed=2 * tokens * top * width, transcendentals=0
        ),
        name="cut_grads",
    )(grads)


def products(grads, slopes):
    return (grads.astype(jnp.float32) * slopes.astype(jnp.float32)).astype(jnp.bfloat16)


def local(acts, hid_grad, routes, probs, w_gate):
    tokens = acts[0]
    n_tokens, width = tokens.shape
    mine = w_gate[0, 0]
    hidden = mine.shape[1]
    core = lax.axis_index("core")
    rows_here = DEVICES * SHARE

    flat_expert = routes[0].reshape(-1)
    pairs = flat_expert.shape[0]
    number = jnp.arange(pairs, dtype=jnp.int32)
    earlier = (flat_expert[:, None] == flat_expert[None, :]) & (number[None, :] < number[:, None])
    slot = jnp.sum(earlier.astype(jnp.int32), axis=1)
    target = flat_expert * SLOTS + slot
    by_token = target.reshape(n_tokens, TOP)

    places = jnp.arange(EXPERTS * SLOTS, dtype=jnp.int32).reshape(EXPERTS, 1, SLOTS)
    places = jnp.broadcast_to(places, (EXPERTS, 2, SLOTS)).reshape(-1)
    row_hit = [places[:, None] == by_token[None, :, k] for k in range(TOP)]
    place_token = (row_hit[0] | row_hit[1]).astype(jnp.bfloat16)
    sent = bf16_dot(place_token, tokens, ((1,), (0,))).astype(jnp.bfloat16)
    rows = exchange(sent.reshape(DEVICES, SHARE, width)).reshape(rows_here, width)

    pieces = [cut(hid_grad[0], h) for h in range(2)]
    halves = [lax.ppermute(piece, "pipe", BACK) for piece in pieces]
    other = lax.ppermute(mine, "core", [(0, 1), (1, 0)])
    lower = jnp.where(core == 0, mine, other)
    upper = jnp.where(core == 0, other, mine)

    first = exchange(place(target, halves[0])).reshape(rows_here, hidden)
    slopes = [after(derivative(bf16_dot(rows, w, ((1,), (0,))))) for w in (lower, upper)]
    target, *slopes = after(target, *slopes)
    placed = place(target, halves[1])
    first, placed = after(first, placed)
    second = exchange(placed).reshape(rows_here, hidden)

    columns = width // COLUMN_PARTS
    early = []
    for j in range(COLUMN_PARTS):
        part = lower[j * columns : (j + 1) * columns]
        term = bf16_dot(products(*after(first, slopes[0])), part, ((1,), (1,)))
        early.append(after(term.astype(jnp.bfloat16)))

    hit = [by_token[:, k, None] == places[None, :] for k in range(TOP)]
    mix = sum(jnp.where(hit[k], probs[0][:, k, None], 0.0) for k in range(TOP))
    high = lax.reduce_precision(mix, 8, 7)
    mix = jnp.concatenate([high, mix - high]).astype(jnp.bfloat16)

    parts = []
    for j in range(COLUMN_PARTS):
        part = upper[j * columns : (j + 1) * columns]
        late = bf16_dot(products(*after(second, slopes[1])), part, ((1,), (1,)))
        term = (early[j].astype(jnp.float32) + late).astype(jnp.bfloat16)
        returned = exchange(term.reshape(DEVICES, SHARE, columns)).reshape(-1, columns)
        both = bf16_dot(mix, returned, ((1,), (0,)))
        summed = (both[:n_tokens] + both[n_tokens:]).astype(jnp.bfloat16)
        parts.append(lax.ppermute(summed, "pipe", BACK))
    return jnp.concatenate(parts, axis=1)[None]


def solution(mesh):
    fine = Mesh(mesh.devices.reshape(4, 4, 2, 2, 2), ("pipe",) + PLANE)
    placed = (
        P("pipe", PLANE, None),
        P("pipe", PLANE, None, None),
        P("pipe", PLANE, None),
        P("pipe", PLANE, None),
        P("pipe", PLANE, None, None),
    )
    return jax.shard_map(
        local, mesh=fine, in_specs=placed, out_specs=P("pipe", PLANE, None), check_vma=False
    )
```

```python
import functools

import jax
import jax.numpy as jnp
from jax import lax
from jax.experimental import pallas as pl
from jax.experimental.pallas import tpu as pltpu
from jax.sharding import Mesh, PartitionSpec as P

EXPERTS = 8
TOP = 2
SLOTS = 64
PLANE = ("z", "xp", "p", "core")
DEVICES = 32
SHARE = SLOTS // 2
BACK = [((i + 1) % 4, i) for i in range(4)]
COLUMN_PARTS = 2
SHARDS = 4
FIRST = 1408
VMEM = 56 * 1024 * 1024


def exchange(block):
    return lax.all_to_all(block, PLANE, split_axis=0, concat_axis=0, tiled=True)


def after(*values):
    return lax.optimization_barrier(values if len(values) > 1 else values[0])


def derivative(gate_pre):
    squash = jax.nn.sigmoid(gate_pre)
    return (squash * (1.0 + gate_pre * (1.0 - squash))).astype(jnp.bfloat16)


def bf16_dot(a, b, dims):
    return lax.dot_general(a, b, (dims, ((), ())), preferred_element_type=jnp.float32)


def place_kernel(target_ref, grads_ref, out_ref):
    tokens, top, columns = grads_ref.shape
    places = lax.broadcasted_iota(jnp.int32, (EXPERTS * SLOTS, tokens * top), 0)
    hit = jnp.where(places == target_ref[...], 1.0, 0.0).astype(jnp.bfloat16)
    grads = grads_ref[...].reshape(tokens * top, columns)
    placed = jnp.dot(hit, grads, preferred_element_type=jnp.float32).astype(jnp.bfloat16)
    out_ref[:, 0] = placed.reshape(EXPERTS, 2, SHARE, columns)


def place(target, grads):
    tokens, top, width = grads.shape
    pairs, hidden = tokens * top, width // 2
    columns = hidden
    steps = 1
    out = pl.pallas_call(
        place_kernel,
        grid=(2, steps),
        in_specs=[
            pl.BlockSpec((1, pairs), lambda p, j: (0, 0)),
            pl.BlockSpec((tokens, top, columns), lambda p, j: (0, 0, p * steps + j)),
        ],
        out_specs=pl.BlockSpec((EXPERTS, 1, 2, SHARE, columns), lambda p, j: (0, p, 0, 0, j)),
        out_shape=jax.ShapeDtypeStruct((EXPERTS, 2, 2, SHARE, hidden), jnp.bfloat16),
        compiler_params=pltpu.CompilerParams(vmem_limit_bytes=VMEM),
        cost_estimate=pl.CostEstimate(
            flops=4 * EXPERTS * SLOTS * pairs * hidden,
            bytes_accessed=4 * (EXPERTS * SLOTS + pairs) * hidden,
            transcendentals=0,
        ),
        name="place_grads",
    )(target.reshape(1, pairs), grads)
    return out.reshape(DEVICES, SHARE, hidden)


def cut_kernel(start, size, in_ref, out_ref, held, sems):
    hidden = in_ref.shape[2] // SHARDS
    arrive, leave = [], []
    for f in range(SHARDS):
        source = in_ref.at[:, :, pl.ds(f * hidden + start, size)]
        target = out_ref.at[:, :, pl.ds(f * size, size)]
        arrive.append(pltpu.make_async_copy(source, held.at[f], sems.at[f]))
        leave.append(pltpu.make_async_copy(held.at[f], target, sems.at[SHARDS + f]))
    for copy in arrive:
        copy.start()
    for f in range(SHARDS):
        arrive[f].wait()
        leave[f].start()
    for copy in leave:
        copy.wait()


def cut(grads, start, size):
    tokens, top, _ = grads.shape
    return pl.pallas_call(
        functools.partial(cut_kernel, start, size),
        in_specs=[pl.BlockSpec(memory_space=pl.ANY)],
        out_specs=pl.BlockSpec(memory_space=pl.ANY),
        out_shape=jax.ShapeDtypeStruct((tokens, top, SHARDS * size), grads.dtype),
        scratch_shapes=[
            pltpu.VMEM((SHARDS, tokens, top, size), grads.dtype),
            pltpu.SemaphoreType.DMA((2 * SHARDS,)),
        ],
        compiler_params=pltpu.CompilerParams(vmem_limit_bytes=VMEM),
        cost_estimate=pl.CostEstimate(
            flops=0, bytes_accessed=4 * tokens * top * SHARDS * size, transcendentals=0
        ),
        name="cut_grads",
    )(grads)


def lay_kernel(core_ref, mine_ref, other_ref, wide_ref, narrow_ref):
    def lay(lower, upper):
        for n, w in enumerate((lower, upper)):
            wide, narrow = FIRST, w.shape[1] - FIRST
            wide_ref[:, n * wide : (n + 1) * wide] = w[:, :wide]
            narrow_ref[:, n * narrow : (n + 1) * narrow] = w[:, wide:]

    @pl.when(core_ref[0] == 0)
    def _():
        lay(mine_ref, other_ref)

    @pl.when(core_ref[0] != 0)
    def _():
        lay(other_ref, mine_ref)


def lay_weights(core, mine, other):
    width, hidden = mine.shape
    block = 256
    sizes = (2 * FIRST, 2 * (hidden - FIRST))
    return pl.pallas_call(
        lay_kernel,
        grid=(width // block,),
        in_specs=[pl.BlockSpec(memory_space=pltpu.SMEM)]
        + [pl.BlockSpec((block, hidden), lambda i: (i, 0))] * 2,
        out_specs=[pl.BlockSpec((block, size), lambda i: (i, 0)) for size in sizes],
        out_shape=[jax.ShapeDtypeStruct((width, size), mine.dtype) for size in sizes],
        compiler_params=pltpu.CompilerParams(vmem_limit_bytes=VMEM),
        cost_estimate=pl.CostEstimate(
            flops=0, bytes_accessed=8 * width * hidden, transcendentals=0
        ),
        name="lay_weights",
    )(core.reshape(1), mine, other)


def products(grads, slopes):
    return (grads.astype(jnp.float32) * slopes.astype(jnp.float32)).astype(jnp.bfloat16)


def local(acts, hid_grad, routes, probs, w_gate):
    tokens = acts[0]
    n_tokens, width = tokens.shape
    mine = w_gate[0, 0]
    hidden = mine.shape[1]
    core = lax.axis_index("core")
    rows_here = DEVICES * SHARE

    flat_expert = routes[0].reshape(-1)
    pairs = flat_expert.shape[0]
    number = jnp.arange(pairs, dtype=jnp.int32)
    earlier = (flat_expert[:, None] == flat_expert[None, :]) & (number[None, :] < number[:, None])
    slot = jnp.sum(earlier.astype(jnp.int32), axis=1)
    target = flat_expert * SLOTS + slot
    by_token = target.reshape(n_tokens, TOP)

    places = jnp.arange(EXPERTS * SLOTS, dtype=jnp.int32).reshape(EXPERTS, 1, SLOTS)
    places = jnp.broadcast_to(places, (EXPERTS, 2, SLOTS)).reshape(-1)
    row_hit = [places[:, None] == by_token[None, :, k] for k in range(TOP)]
    place_token = (row_hit[0] | row_hit[1]).astype(jnp.bfloat16)
    sent = bf16_dot(place_token, tokens, ((1,), (0,))).astype(jnp.bfloat16)
    rows = exchange(sent.reshape(DEVICES, SHARE, width)).reshape(rows_here, width)

    pieces = [cut(hid_grad[0], 0, FIRST), cut(hid_grad[0], FIRST, hidden - FIRST)]
    halves = [lax.ppermute(piece, "pipe", BACK) for piece in pieces]
    other = lax.ppermute(mine, "core", [(0, 1), (1, 0)])
    weights = lay_weights(core, mine, other)

    target, *weights = after(target, *weights)
    first = exchange(place(target, halves[0])).reshape(rows_here, 2 * FIRST)
    slopes = [after(derivative(bf16_dot(rows, w, ((1,), (0,))))) for w in weights]
    target, *slopes = after(target, *slopes)
    placed = place(target, halves[1])
    first, placed = after(first, placed)
    second = exchange(placed).reshape(rows_here, 2 * (hidden - FIRST))

    columns = width // COLUMN_PARTS
    early = []
    for j in range(COLUMN_PARTS):
        part = weights[0][j * columns : (j + 1) * columns]
        term = bf16_dot(products(*after(first, slopes[0])), part, ((1,), (1,)))
        early.append(after(term.astype(jnp.bfloat16)))

    hit = [by_token[:, k, None] == places[None, :] for k in range(TOP)]
    mix = sum(jnp.where(hit[k], probs[0][:, k, None], 0.0) for k in range(TOP))
    high = lax.reduce_precision(mix, 8, 7)
    mix = jnp.concatenate([high, mix - high]).astype(jnp.bfloat16)

    parts = []
    for j in range(COLUMN_PARTS):
        part = weights[1][j * columns : (j + 1) * columns]
        late = bf16_dot(products(*after(second, slopes[1])), part, ((1,), (1,)))
        term = (early[j].astype(jnp.float32) + late).astype(jnp.bfloat16)
        returned = exchange(term.reshape(DEVICES, SHARE, columns)).reshape(-1, columns)
        both = bf16_dot(mix, returned, ((1,), (0,)))
        summed = (both[:n_tokens] + both[n_tokens:]).astype(jnp.bfloat16)
        parts.append(lax.ppermute(summed, "pipe", BACK))
    return jnp.concatenate(parts, axis=1)[None]


def solution(mesh):
    fine = Mesh(mesh.devices.reshape(4, 4, 2, 2, 2), ("pipe",) + PLANE)
    placed = (
        P("pipe", PLANE, None),
        P("pipe", PLANE, None, None),
        P("pipe", PLANE, None),
        P("pipe", PLANE, None),
        P("pipe", PLANE, None, None),
    )
    return jax.shard_map(
        local, mesh=fine, in_specs=placed, out_specs=P("pipe", PLANE, None), check_vma=False
    )
```

```python
import functools

import jax
import jax.numpy as jnp
from jax import lax
from jax.experimental import pallas as pl
from jax.experimental.pallas import tpu as pltpu
from jax.sharding import Mesh, PartitionSpec as P

EXPERTS = 8
TOP = 2
SLOTS = 64
PLANE = ("z", "xp", "p", "core")
DEVICES = 32
SHARE = SLOTS // 2
BACK = [((i + 1) % 4, i) for i in range(4)]
COLUMN_PARTS = 2
SHARDS = 4
FIRST = 1408
VMEM = 56 * 1024 * 1024


def exchange(block):
    return lax.all_to_all(block, PLANE, split_axis=0, concat_axis=0, tiled=True)


def after(*values):
    return lax.optimization_barrier(values if len(values) > 1 else values[0])


def derivative(gate_pre):
    squash = jax.nn.sigmoid(gate_pre)
    return (squash * (1.0 + gate_pre * (1.0 - squash))).astype(jnp.bfloat16)


def bf16_dot(a, b, dims):
    return lax.dot_general(a, b, (dims, ((), ())), preferred_element_type=jnp.float32)


def place_kernel(target_ref, grads_ref, out_ref):
    tokens, top, columns = grads_ref.shape
    places = lax.broadcasted_iota(jnp.int32, (EXPERTS * SLOTS, tokens * top), 0)
    hit = jnp.where(places == target_ref[...], 1.0, 0.0).astype(jnp.bfloat16)
    grads = grads_ref[...].reshape(tokens * top, columns)
    placed = jnp.dot(hit, grads, preferred_element_type=jnp.float32).astype(jnp.bfloat16)
    out_ref[:, 0] = placed.reshape(EXPERTS, 2, SHARE, columns)


def place(target, grads):
    tokens, top, width = grads.shape
    pairs, hidden = tokens * top, width // 2
    columns = hidden
    steps = 1
    out = pl.pallas_call(
        place_kernel,
        grid=(2, steps),
        in_specs=[
            pl.BlockSpec((1, pairs), lambda p, j: (0, 0)),
            pl.BlockSpec((tokens, top, columns), lambda p, j: (0, 0, p * steps + j)),
        ],
        out_specs=pl.BlockSpec((EXPERTS, 1, 2, SHARE, columns), lambda p, j: (0, p, 0, 0, j)),
        out_shape=jax.ShapeDtypeStruct((EXPERTS, 2, 2, SHARE, hidden), jnp.bfloat16),
        compiler_params=pltpu.CompilerParams(vmem_limit_bytes=VMEM),
        cost_estimate=pl.CostEstimate(
            flops=4 * EXPERTS * SLOTS * pairs * hidden,
            bytes_accessed=4 * (EXPERTS * SLOTS + pairs) * hidden,
            transcendentals=0,
        ),
        name="place_grads",
    )(target.reshape(1, pairs), grads)
    return out.reshape(DEVICES, SHARE, hidden)


def cut_kernel(start, size, in_ref, out_ref, held, sems):
    hidden = in_ref.shape[2] // SHARDS
    arrive, leave = [], []
    for f in range(SHARDS):
        source = in_ref.at[:, :, pl.ds(f * hidden + start, size)]
        target = out_ref.at[:, :, pl.ds(f * size, size)]
        arrive.append(pltpu.make_async_copy(source, held.at[f], sems.at[f]))
        leave.append(pltpu.make_async_copy(held.at[f], target, sems.at[SHARDS + f]))
    for copy in arrive:
        copy.start()
    for f in range(SHARDS):
        arrive[f].wait()
        leave[f].start()
    for copy in leave:
        copy.wait()


def cut(grads, start, size):
    tokens, top, _ = grads.shape
    return pl.pallas_call(
        functools.partial(cut_kernel, start, size),
        in_specs=[pl.BlockSpec(memory_space=pl.ANY)],
        out_specs=pl.BlockSpec(memory_space=pl.ANY),
        out_shape=jax.ShapeDtypeStruct((tokens, top, SHARDS * size), grads.dtype),
        scratch_shapes=[
            pltpu.VMEM((SHARDS, tokens, top, size), grads.dtype),
            pltpu.SemaphoreType.DMA((2 * SHARDS,)),
        ],
        compiler_params=pltpu.CompilerParams(vmem_limit_bytes=VMEM),
        cost_estimate=pl.CostEstimate(
            flops=0, bytes_accessed=4 * tokens * top * SHARDS * size, transcendentals=0
        ),
        name="cut_grads",
    )(grads)


def lay_kernel(core_ref, mine_ref, other_ref, wide_ref, narrow_ref):
    def lay(lower, upper):
        for n, w in enumerate((lower, upper)):
            wide, narrow = FIRST, w.shape[1] - FIRST
            wide_ref[:, n * wide : (n + 1) * wide] = w[:, :wide]
            narrow_ref[:, n * narrow : (n + 1) * narrow] = w[:, wide:]

    @pl.when(core_ref[0] == 0)
    def _():
        lay(mine_ref, other_ref)

    @pl.when(core_ref[0] != 0)
    def _():
        lay(other_ref, mine_ref)


def lay_weights(core, mine, other):
    width, hidden = mine.shape
    block = 256
    sizes = (2 * FIRST, 2 * (hidden - FIRST))
    return pl.pallas_call(
        lay_kernel,
        grid=(width // block,),
        in_specs=[pl.BlockSpec(memory_space=pltpu.SMEM)]
        + [pl.BlockSpec((block, hidden), lambda i: (i, 0))] * 2,
        out_specs=[pl.BlockSpec((block, size), lambda i: (i, 0)) for size in sizes],
        out_shape=[jax.ShapeDtypeStruct((width, size), mine.dtype) for size in sizes],
        compiler_params=pltpu.CompilerParams(vmem_limit_bytes=VMEM),
        cost_estimate=pl.CostEstimate(
            flops=0, bytes_accessed=8 * width * hidden, transcendentals=0
        ),
        name="lay_weights",
    )(core.reshape(1), mine, other)


def products(grads, slopes):
    return (grads.astype(jnp.float32) * slopes.astype(jnp.float32)).astype(jnp.bfloat16)


def local(acts, hid_grad, routes, probs, w_gate):
    tokens = acts[0]
    n_tokens, width = tokens.shape
    mine = w_gate[0, 0]
    hidden = mine.shape[1]
    core = lax.axis_index("core")
    rows_here = DEVICES * SHARE

    flat_expert = routes[0].T.reshape(-1)
    pairs = flat_expert.shape[0]
    number = jnp.arange(pairs, dtype=jnp.int32)
    earlier = (flat_expert[:, None] == flat_expert[None, :]) & (number[None, :] < number[:, None])
    slot = jnp.sum(earlier.astype(jnp.int32), axis=1)
    by_route = (flat_expert * SLOTS + slot).reshape(TOP, n_tokens)
    target = by_route.T.reshape(-1)

    places = jnp.arange(EXPERTS * SLOTS, dtype=jnp.int32).reshape(EXPERTS, 1, SLOTS)
    places = jnp.broadcast_to(places, (EXPERTS, 2, SLOTS)).reshape(-1)
    row_hit = [places[:, None] == by_route[None, k] for k in range(TOP)]
    place_token = (row_hit[0] | row_hit[1]).astype(jnp.bfloat16)
    sent = bf16_dot(place_token, tokens, ((1,), (0,))).astype(jnp.bfloat16)
    rows = exchange(sent.reshape(DEVICES, SHARE, width)).reshape(rows_here, width)

    pieces = [cut(hid_grad[0], 0, FIRST), cut(hid_grad[0], FIRST, hidden - FIRST)]
    halves = [lax.ppermute(piece, "pipe", BACK) for piece in pieces]
    other = lax.ppermute(mine, "core", [(0, 1), (1, 0)])
    weights = lay_weights(core, mine, other)

    target, *weights = after(target, *weights)
    first = exchange(place(target, halves[0])).reshape(rows_here, 2 * FIRST)
    slopes = [after(derivative(bf16_dot(rows, w, ((1,), (0,))))) for w in weights]
    target, *slopes = after(target, *slopes)
    placed = place(target, halves[1])
    first, placed = after(first, placed)
    second = exchange(placed).reshape(rows_here, 2 * (hidden - FIRST))

    columns = width // COLUMN_PARTS
    early = []
    for j in range(COLUMN_PARTS):
        part = weights[0][j * columns : (j + 1) * columns]
        term = bf16_dot(products(*after(first, slopes[0])), part, ((1,), (1,)))
        early.append(after(term.astype(jnp.bfloat16)))

    hit = [by_route[k, :, None] == places[None, :] for k in range(TOP)]
    mix = sum(jnp.where(hit[k], probs[0][:, k, None], 0.0) for k in range(TOP))
    high = lax.reduce_precision(mix, 8, 7)
    mix = jnp.concatenate([high, mix - high]).astype(jnp.bfloat16)

    parts = []
    for j in range(COLUMN_PARTS):
        part = weights[1][j * columns : (j + 1) * columns]
        late = bf16_dot(products(*after(second, slopes[1])), part, ((1,), (1,)))
        term = (early[j].astype(jnp.float32) + late).astype(jnp.bfloat16)
        returned = exchange(term.reshape(DEVICES, SHARE, columns)).reshape(-1, columns)
        both = bf16_dot(mix, returned, ((1,), (0,)))
        summed = (both[:n_tokens] + both[n_tokens:]).astype(jnp.bfloat16)
        parts.append(lax.ppermute(summed, "pipe", BACK))
    return jnp.concatenate(parts, axis=1)[None]


def solution(mesh):
    fine = Mesh(mesh.devices.reshape(4, 4, 2, 2, 2), ("pipe",) + PLANE)
    placed = (
        P("pipe", PLANE, None),
        P("pipe", PLANE, None, None),
        P("pipe", PLANE, None),
        P("pipe", PLANE, None),
        P("pipe", PLANE, None, None),
    )
    return jax.shard_map(
        local, mesh=fine, in_specs=placed, out_specs=P("pipe", PLANE, None), check_vma=False
    )
```
